128 devices in a mesh: row: 16 (over x, z), col: 8 (over y, core).
Axes of the slice: x: 4, y: 4, z: 4, core: 2. Of those that a mesh axis runs over, the one named last changes fastest.
Arguments:
- root_inverse: float32 [2, 2048, 4, 1024], P(None, 'row', None, 'col'), as said below
- child_coupling: float32 [2, 2, 2048, 2, 1024], P(None, None, 'row', None, 'col'), may hold values from -0.046875 to 0.046875
- child_inverse: float32 [2, 1, 2048, 2, 1024], P(None, None, 'row', None, 'col'), as said below
- pattern: int32 [2, 32], replicated, may hold values 0 or 1
Outputs:
- sigma_root: float32 [2, 2048, 4, 1024], P(None, 'row', None, 'col')
- sigma_coupling: float32 [2, 2, 2048, 2, 1024], P(None, None, 'row', None, 'col')
- sigma_child: float32 [2, 128, 2, 1024], P(None, None, None, 'col')
The draws below stay inside these ranges and needn't reach their ends.
Inputs may be any that keep to these rules, and one draw needn't show every extreme that they name: `root_inverse`: read row-major as a 4096 x 4096 matrix it is lower triangular with a positive diagonal. `child_inverse`: read row-major each child's 2048 x 2048 matrix is lower triangular with a positive diagonal. `pattern`: 1 where child j's separator couples to root supernode i, else 0.
All inputs are finite; a program needn't handle non-finite values.
Results may differ from the reference program's by a relative error of at most 0.00013.
Values sent between devices are 32-bit elements; how exact they have to be, the bound alone decides.
No kernel may reach another device: no remote copies, remote signals or barrier semaphores. Data moves between devices by JAX's collectives and lax.ppermute only.
A program may use at most 128 MiB of HBM per device.

```python
import jax
import jax.numpy as jnp
from jax import lax

B = 128
NR = 4096
NC = 2048
CH = 2
NRB = 32
RBD = 2
RCD = 4
CRD = 1
CCD = 2
N_ROW = 16
N_COL = 8


def lower_factor(key, order):
    key_off, key_diag = jax.random.split(key, 2)
    off_values = jax.random.normal(key_off, (order, order), jnp.float32)
    off_values = off_values * (1.0 / order ** 0.5)
    diagonal = jax.random.uniform(key_diag, (order,), jnp.float32, 0.5, 1.5)
    row_index = jnp.arange(order)[:, None]
    col_index = jnp.arange(order)[None, :]
    lower = jnp.where(row_index > col_index, off_values, 0.0)
    return lower + jnp.where(row_index == col_index, diagonal[:, None], 0.0)


def draw_root_inverse(key, part):
    matrix = lower_factor(jax.random.fold_in(key, 11), NR)
    return matrix.reshape(RBD, N_ROW * B, RCD, N_COL * B)


def draw_child_inverse(key, part):
    keys = jax.random.split(jax.random.fold_in(key, 23), CH)
    matrices = jnp.stack([lower_factor(keys[index], NC) for index in range(CH)])
    return matrices.reshape(CH, CRD, N_ROW * B, CCD, N_COL * B)


def touch_ends(entries, key, least, top_value):
    place = [jax.random.randint(jax.random.fold_in(key, axis), (), 0, length) for axis, length in enumerate(entries.shape)]
    longest = entries.shape.index(max(entries.shape))
    beside = place[:longest] + [(place[longest] + 1) % entries.shape[longest]] + place[longest + 1:]
    return entries.at[tuple(place)].set(least).at[tuple(beside)].set(top_value)


def levels(stream_key, dims, pieces, least, top_value):
    factor_of, own = 1.0, jax.random.fold_in(stream_key, 6)
    for dim, parts in pieces:
        heights = jnp.exp(jax.random.uniform(jax.random.fold_in(own, dim), (parts,), jnp.float32, least / len(pieces), top_value / len(pieces)))
        factor_of = factor_of * jnp.repeat(heights, dims[dim] // parts).reshape([-1 if axis == dim else 1 for axis in range(len(dims))])
    return factor_of


def gaussian(stream_key, shape, deviation, limit, shards=(), dtype=jnp.bfloat16):
    entries = deviation * jax.random.normal(stream_key, shape, jnp.float32)
    if shards:
        entries = entries * levels(stream_key, shape, shards, -0.22, 0.18)
    return jnp.clip(entries, -limit, limit).astype(dtype)


def setup_inputs(seed: int = 0) -> dict:
    streams_of = jax.random.split(jax.random.key(seed), 5)
    root_inverse = draw_root_inverse(jax.random.fold_in(streams_of[4], 71), 0)
    child_coupling = gaussian(streams_of[1], (CH, RBD, N_ROW * B, CCD, N_COL * B), (4 * NR) ** -0.5, 0.046875, ((2, 16), (4, 8)), jnp.float32)
    child_inverse = draw_child_inverse(jax.random.fold_in(streams_of[4], 71), 0)
    pattern = touch_ends((jax.random.randint(streams_of[3], (CH, NRB), 0, 2) < 1).astype(jnp.int32), jax.random.fold_in(streams_of[3], 1), 0, 1)
    return {"root_inverse": root_inverse, "child_coupling": child_coupling, "child_inverse": child_inverse, "pattern": pattern}


def reference(root_inverse, child_coupling, child_inverse, pattern):
    highest = lax.Precision.HIGHEST
    root_matrix = root_inverse.reshape(NR, NR)
    sigma_root = jnp.einsum('ki,kj->ij', root_matrix, root_matrix, precision=highest)
    keep = jnp.repeat(pattern.astype(jnp.float32), B, axis=1)
    coupling = child_coupling.reshape(CH, NR, NC) * keep[:, :, None]
    child_matrix = child_inverse.reshape(CH, NC, NC)
    update = jnp.einsum('jik,jkn->jin', coupling, child_matrix, precision=highest)
    product = jnp.einsum('ik,jkn->jin', sigma_root, update, precision=highest)
    sigma_coupling = -(keep[:, :, None] * product)
    child_blocks = NC // B
    child_split = child_matrix.reshape(CH, NC, child_blocks, B)
    first_part = jnp.einsum('jkcr,jkcs->jcrs', child_split, child_split, precision=highest)
    update_split = update.reshape(CH, NR, child_blocks, B)
    coupling_split = sigma_coupling.reshape(CH, NR, child_blocks, B)
    second_part = jnp.einsum('jkcr,jkcs->jcrs', update_split, coupling_split, precision=highest)
    diagonal_blocks = first_part - second_part
    diagonal_blocks = diagonal_blocks.reshape(CH, CCD, N_COL, B, B).transpose(0, 3, 1, 2, 4).reshape(CH, B, CCD, N_COL * B)
    return (sigma_root.reshape(RBD, N_ROW * B, RCD, N_COL * B),
            sigma_coupling.reshape(CH, RBD, N_ROW * B, CCD, N_COL * B),
            diagonal_blocks)
```

```python
import functools

import jax
import jax.numpy as jnp
from jax import lax
from jax.experimental import pallas as pl
from jax.experimental.pallas import tpu as pltpu
from jax.sharding import PartitionSpec as P

X, Z, Y, CORES = 4, 4, 4, 2
W = 128
F32, BF16 = jnp.float32, jnp.bfloat16
AXES = ("row", "col")


def moves(target):
    pairs = []
    for x in range(X):
        for z in range(Z):
            for y in range(Y):
                for core in range(CORES):
                    there = target(x, z, y, core)
                    if there is not None:
                        u, w, v, k = there
                        pairs.append((((x * Z + z) * Y + y) * CORES + core, (((u % X) * Z + w % Z) * Y + v % Y) * CORES + k))
    return pairs


def way(core):
    return 1 - 2 * core


ALONG_X = moves(lambda x, z, y, k: (x + way(k), z, y, k))
ALONG_Z = moves(lambda x, z, y, k: (x, z + way(k), y, k))
ALONG_Y = moves(lambda x, z, y, k: (x, z, y + way(k), k))
SWAP = moves(lambda x, z, y, k: (x, z, y, 1 - k))
FOLD = moves(lambda x, z, y, k: (3 - x, z, y, k) if x >= 2 else None)


def mirror(first):
    def target(x, z, y, k):
        r, c = x * Z + z, y * CORES + k
        to = c if (r % 2 == 0) == first else c + 8
        return to // Z, to % Z, (r // 2) // CORES, (r // 2) % CORES

    return moves(target)


MIRROR_1, MIRROR_2 = mirror(True), mirror(False)


def send(value, pairs):
    return lax.ppermute(value, AXES, pairs)


def ring(value, pairs):
    parts = [value]
    for _ in range(3):
        parts.append(send(parts[-1], pairs))
    return parts


def gather(value, first, second):
    return ring(jnp.concatenate(ring(value, first), axis=0), second)


def share(value):
    mine = ring(value, ALONG_Y)
    return mine + [send(part, SWAP) for part in mine]


def place():
    row, col = lax.axis_index("row"), lax.axis_index("col")
    core = col % 2
    return row // 4, row % 4, col // 2, core, 1 - 2 * core


def column_of(w, y, core, d):
    if w < 4:
        return 2 * ((y - w * d + 8) % 4) + core
    return 2 * ((y + (w - 4) * d + 8) % 4) + 1 - core


def steps(r, x, z, d):
    return ((x - r // 4) * d + 8) % 4, ((z - r % 4) * d + 8) % 4


def at(index, size):
    return pl.ds(pl.multiple_of(index * size, size), size)


def split(value):
    high = value.astype(BF16)
    return high, (value - high.astype(F32)).astype(BF16)


def dot3(left, right, dims=((1,), (0,))):
    dot = functools.partial(lax.dot_general, dimension_numbers=(dims, ((), ())), preferred_element_type=F32)
    return dot(left[0], right[0]) + (dot(left[0], right[1]) + dot(left[1], right[0]))


def call(kernel, outs, scratch=(), smem_first=False, count=0, flops=0, vmem=24):
    in_specs = [pl.BlockSpec(memory_space=pltpu.VMEM)] * count
    if smem_first:
        in_specs = [pl.BlockSpec(memory_space=pltpu.SMEM)] + in_specs
    return pl.pallas_call(
        kernel,
        out_shape=outs,
        in_specs=in_specs,
        out_specs=jax.tree.map(lambda _: pl.BlockSpec(memory_space=pltpu.VMEM), outs),
        scratch_shapes=list(scratch),
        compiler_params=pltpu.CompilerParams(vmem_limit_bytes=vmem << 20),
        cost_estimate=pl.CostEstimate(flops=flops, bytes_accessed=1 << 22, transcendentals=0),
    )


def shape(*dims, dtype=F32):
    return jax.ShapeDtypeStruct(dims, dtype)


def cut_kernel(pattern, a, c, k, x1, x2, fold, keep_own, z1, cw, m1, m2):
    row = lax.axis_index("row")

    def block_a(i, q):
        return a[pl.ds(i * 512 + q, W, stride=4), :]

    def block_k(j, q):
        return k[pl.ds(j * 256 + q, W, stride=2), :]

    for q in range(3):
        x1[:, q * W : (q + 1) * W] = block_a(1, q)
    x2[...] = block_a(0, 0)
    fold[:, :W] = block_a(0, 1)
    fold[:, W:] = block_k(0, 1)
    keep_own[:, :W] = block_a(1, 3)
    keep_own[:, W:] = block_k(1, 1)
    for j in range(2):
        z1[:, j * W : (j + 1) * W] = block_k(j, 0)
        for i in range(2):
            kept = pattern[j, row + 16 * i].astype(F32)
            for q in range(2):
                block = c[pl.ds((j * 2 + i) * 256 + q, W, stride=2), :]
                cw[pl.ds((j * 2 + i) * W, W), q * W : (q + 1) * W] = block * kept
    even = row % 2 == 0
    for m, (i, q) in enumerate(((0, 0), (1, 0), (1, 2))):
        low, high = block_a(i, q).T, block_a(i, q + 1).T
        m1[pl.ds(m * W, W), :] = jnp.where(even, low, high)
        m2[pl.ds(m * W, W), :] = jnp.where(even, high, low)


def update_kernel(*refs):
    cw, z1, e = refs[:8], refs[8:12], refs[12:16]
    outs, (high, low, acc) = refs[16:20], refs[20:]
    x, z, y, core, d = place()
    for w in range(8):
        column = column_of(w, y, core, d)
        for q in range(2):
            t, s = steps(column + 8 * q, x, z, d)
            for j in range(2):
                h, l = split(cw[w][pl.ds(j * 256, 256), q * W : (q + 1) * W])
                high[j, :, at(4 * t + s, W)] = h
                low[j, :, at(4 * t + s, W)] = l
    acc[...] = jnp.zeros_like(acc)
    for t in range(4):
        right = split(z1[t][...])
        for j in range(2):
            part = pl.ds(t * 512, 512)
            acc[j, :, :W] += dot3((high[j, :, part], low[j, :, part]), [v[:, j * W : (j + 1) * W] for v in right])
        from_x = (x - t * d + 8) % 4
        low_x = from_x < 2
        j = jnp.where(low_x, 0, 1)
        part = at(jnp.where(low_x, ((x - 3 + from_x) * d + 8) % 4, t), 512)
        acc[j, :, W:] += dot3((high[j, :, part], low[j, :, part]), split(e[t][:, W:]))
    for j in range(2):
        for i in range(2):
            outs[2 * j + i][...] = acc[j, pl.ds(i * W, W), :]


def root_kernel(*refs):
    m, x1, x2, e = refs[:8], refs[8:12], refs[12:16], refs[16:20]
    (s_out, root_out), (h0, l0, h1, l1) = refs[20:22], refs[22:]
    x, z, y, core, d = place()
    upper = (4 * x + z >= 8).astype(jnp.int32)
    for w in range(8):
        column = column_of(w, y, core, d)
        for n in range(2):
            row = 2 * column + (n + upper) % 2
            s, t = steps(row, x, z, d)
            here = at(4 * t + s, W)
            for part, (hr, lr, lo) in enumerate(((h0, l0, 0), (h1, l1, 0), (h1, l1, W))):
                h, l = split(m[w][pl.ds((n * 3 + part) * W, W), :])
                hr[pl.ds(lo, W), here] = h
                lr[pl.ds(lo, W), here] = l
    s_out[...] = jnp.zeros_like(s_out)
    for t in range(4):
        part = pl.ds(t * 512, 512)
        s_out[:, :384] += dot3((h1[:, part], l1[:, part]), split(x1[t][...]))
        s_out[:W, :W] += dot3((h0[:, part], l0[:, part]), split(x2[t][...]))
        from_x = (x - t * d + 8) % 4

        @pl.when(from_x >= 2)
        def _():
            for s in range(4):
                k = pl.ds((4 * s + t) * W, W)
                s_out[:, 384:] += dot3((h1[:, k], l1[:, k]), split(e[t][pl.ds(s * W, W), :W]))

        @pl.when(from_x < 2)
        def _():
            other = ((x - 3 + from_x) * d + 8) % 4
            for s in range(4):
                k = at(4 * s + other, W)
                s_out[:W, W : 2 * W] += dot3((h0[:, k], l0[:, k]), split(e[t][pl.ds(s * W, W), :W]))

    for i in range(2):
        for q in range(4):
            root_out[pl.ds(i * 512 + q, W, stride=4), :] = s_out[pl.ds(i * W, W), q * W : (q + 1) * W]


def order_kernel(*refs):
    s_in, (high, low) = refs[:8], refs[8:]
    x, z, y, core, d = place()
    for w in range(8):
        column = column_of(w, y, core, d)
        for q in range(4):
            along_x, along_z = steps(column + 8 * (q % 2), x, z, d)
            place_of = 4 * along_z + along_x if q < 2 else 16 + 4 * along_x + along_z
            h, l = split(s_in[w][:, q * W : (q + 1) * W])
            high[:, at(place_of, W)] = h
            low[:, at(place_of, W)] = l


def product_kernel(j, pattern, high, low, *refs):
    pieces, (u0, u1, k), (p_out, g_out) = refs[:8], refs[8:11], refs[11:13]
    row = lax.axis_index("row")
    total = jnp.zeros((256, 256), F32)
    for n in range(8):
        part = pl.ds(n * 512, 512)
        total = total + dot3((high[:, part], low[:, part]), split(pieces[n][...]))
    scaled = [total[i * W : (i + 1) * W] * -pattern[j, row + 16 * i].astype(F32) for i in range(2)]
    for q in range(2):
        cols = slice(q * W, (q + 1) * W)
        own = k[pl.ds(j * 256 + q, W, stride=2), :]
        pair = split(own.T), split(own)
        block = dot3(*pair)
        for i, u in enumerate((u0, u1)):
            p_out[pl.ds(i * 256 + q, W, stride=2), :] = scaled[i][:, cols]
            block = block - dot3(split(u[:, cols].T), split(scaled[i][:, cols]))
        g_out[pl.ds(q * W, W), :] = block


def local(root_inverse, child_coupling, child_inverse, pattern):
    a = root_inverse.reshape(1024, W)
    c = child_coupling.reshape(1024, W)
    k = child_inverse.reshape(512, W)
    x1, x2, fold, keep_own, z1, cw, m1, m2 = call(
        cut_kernel,
        (shape(W, 384), shape(W, W), shape(W, 256), shape(W, 256), shape(W, 256), shape(512, 256), shape(384, W), shape(384, W)),
        smem_first=True,
        count=3,
    )(pattern, a, c, k)

    folded = send(fold, FOLD)
    z2 = jnp.where(lax.axis_index("row") >= 8, keep_own, folded)
    child_parts = gather(z1, ALONG_Z, ALONG_X)
    root_parts = gather(x1, ALONG_X, ALONG_Z)
    coupling_parts = share(cw)
    fold_parts = gather(z2, ALONG_Z, ALONG_X)
    corner_parts = gather(x2, ALONG_X, ALONG_Z)
    mirrored = share(jnp.concatenate([send(m1, MIRROR_1), send(m2, MIRROR_2)], axis=0))

    u = call(
        update_kernel,
        (shape(W, 256),) * 4,
        scratch=[pltpu.VMEM((2, 256, 2048), BF16)] * 2 + [pltpu.VMEM((2, 256, 256), F32)],
        count=16,
        flops=1 << 31,
    )(*coupling_parts, *child_parts, *fold_parts)
    sigma, sigma_root = call(
        root_kernel,
        (shape(256, 512), shape(1024, W)),
        scratch=[pltpu.VMEM((W, 2048), BF16)] * 2 + [pltpu.VMEM((256, 2048), BF16)] * 2,
        count=20,
        flops=1 << 31,
    )(*mirrored, *root_parts, *corner_parts, *fold_parts)
    high, low = call(order_kernel, (shape(256, 4096, dtype=BF16),) * 2, count=8, flops=1 << 20)(*share(sigma))

    products, diagonals = [], []
    for j in range(2):
        u0, u1 = u[2 * j], u[2 * j + 1]
        pieces = gather(u0, ALONG_X, ALONG_Z) + gather(u1, ALONG_Z, ALONG_X)
        p, g = call(
            functools.partial(product_kernel, j),
            (shape(512, W), shape(256, W)),
            smem_first=True,
            count=13,
            flops=1 << 31,
        )(pattern, high, low, *pieces, u0, u1, k)
        terms = lax.all_to_all(g.reshape(16, 16, W), "row", 0, 0)
        mine = jnp.broadcast_to(jnp.sum(terms, axis=0)[None], (16, 16, W))
        diagonals.append(lax.all_to_all(mine, "row", 0, 0).reshape(2, W, W))
        products.append(p)
    sigma_child = jnp.stack(diagonals).transpose(0, 2, 1, 3)
    return (
        sigma_root.reshape(2, W, 4, W),
        jnp.stack(products).reshape(2, 2, W, 2, W),
        sigma_child,
    )


def solution(mesh):
    in_specs = (
        P(None, "row", None, "col"),
        P(None, None, "row", None, "col"),
        P(None, None, "row", None, "col"),
        P(),
    )
    out_specs = (
        P(None, "row", None, "col"),
        P(None, None, "row", None, "col"),
        P(None, None, None, "col"),
    )
    return jax.shard_map(local, mesh=mesh, in_specs=in_specs, out_specs=out_specs, check_vma=False)
```

```python
import functools

import jax
import jax.numpy as jnp
from jax import lax
from jax.experimental import pallas as pl
from jax.experimental.pallas import tpu as pltpu
from jax.sharding import PartitionSpec as P

X, Z, Y, CORES = 4, 4, 4, 2
W = 128
F32, BF16 = jnp.float32, jnp.bfloat16
AXES = ("row", "col")


def moves(target):
    pairs = []
    for x in range(X):
        for z in range(Z):
            for y in range(Y):
                for core in range(CORES):
                    there = target(x, z, y, core)
                    if there is not None:
                        u, w, v, k = there
                        pairs.append((((x * Z + z) * Y + y) * CORES + core, ((u * Z + w) * Y + v) * CORES + k))
    return pairs


ALONG_X = [moves(lambda x, z, y, k, n=n: ((x + n * (1 - 2 * k)) % X, z, y, k)) for n in (1, -1)]
ALONG_Z = [moves(lambda x, z, y, k, n=n: (x, (z + n * (1 - 2 * k)) % Z, y, k)) for n in (1, -1)]
FLIP_X = [moves(lambda x, z, y, k, n=n: (x ^ (n if k == 0 else 4 - n), z, y, k)) for n in (1, 3)]
FLIP_Z = [moves(lambda x, z, y, k, n=n: (x, z ^ (n if k == 0 else 4 - n), y, k)) for n in (1, 3)]
FOLD = moves(lambda x, z, y, k: (3 - x, z, y, k) if x >= 2 else None)


def mirror(first):
    def target(x, z, y, k):
        r, c = x * Z + z, y * CORES + k
        to = c if (r % 2 == 0) == first else c + 8
        return to // Z, to % Z, (r // 2) // CORES, (r // 2) % CORES

    return moves(target)


MIRROR_1, MIRROR_2 = mirror(True), mirror(False)


def send(value, pairs):
    return lax.ppermute(value, AXES, pairs)


def after(value, *others):
    return lax.optimization_barrier((value, *others))[0]


def ring(value, pairs, *others):
    near = send(value, pairs[0])
    return [value, near, send(value, pairs[1]), send(after(near, *others) if others else near, pairs[0])]


def stack_kernel(*refs):
    sources, outs, semaphores = refs[:8], refs[8:10], refs[10]
    rows = sources[0].shape[0]
    copies = [
        pltpu.make_async_copy(source, outs[n // 4].at[pl.ds((n % 4) * rows, rows)], semaphores.at[n]) for n, source in enumerate(sources)
    ]
    for copy in copies:
        copy.start()
    for copy in copies:
        copy.wait()


def gather(value_x, value_z, *others):
    rings = ring(value_x, ALONG_X, *others) + ring(value_z, ALONG_Z, *others)
    four_x, four_z = pl.pallas_call(
        stack_kernel,
        out_shape=(shape(4 * value_x.shape[0], value_x.shape[1]),) * 2,
        in_specs=[pl.BlockSpec(memory_space=pl.ANY)] * 8,
        out_specs=(pl.BlockSpec(memory_space=pltpu.VMEM),) * 2,
        scratch_shapes=[pltpu.SemaphoreType.DMA((8,))],
        compiler_params=pltpu.CompilerParams(vmem_limit_bytes=8 << 20),
    )(*rings)
    return ring(four_x, ALONG_Z), ring(four_z, ALONG_X), four_x


def place():
    row, core = lax.axis_index("row"), lax.axis_index("col") % 2
    return row // 4, row % 4, 1 - 2 * core


def origin(index, step, d):
    return (index + 4 + (0, -d, d, 2)[step]) % 4


def step_of(there, here, d):
    offset = ((there - here) * d + 8) % 4
    return jnp.where(offset == 3, 1, jnp.where(offset == 0, 0, offset + 1))


def at(index, size):
    return pl.ds(pl.multiple_of(index * size, size), size)


def split(value):
    high = value.astype(BF16)
    return high, (value - high.astype(F32)).astype(BF16)


def put(high, low, where, value):
    h, l = split(value)
    high[where] = h
    low[where] = l


def dot3(left, right):
    dot = functools.partial(jnp.dot, preferred_element_type=F32)
    return dot(left[0], right[0]) + (dot(left[0], right[1]) + dot(left[1], right[0]))


class Staged:
    def __init__(self, source, buffer, semaphore):
        self.copy, self.buffer, self.shape, self.here = pltpu.make_async_copy(source, buffer, semaphore), buffer, buffer.shape, False
        self.copy.start()

    def __getitem__(self, where):
        if not self.here:
            self.copy.wait()
            self.here = True
        return self.buffer[where]


def call(kernel, outs, operands, scratch=(), scalars=(), flops=0, vmem=56):
    operands = [v if isinstance(v, tuple) else (v, None) for v in operands]
    ranges, operands = [v[1] for v in operands], [v[0] for v in operands]
    shapes = [v.shape if cols is None else (v.shape[0], cols[1] - cols[0]) for v, cols in zip(operands, ranges)]
    n, m = len(scalars), len(operands)

    def body(*refs):
        first, sources, rest = refs[:n], refs[n : n + m], refs[n + m :]
        results, rest = rest[: len(outs)], rest[len(outs) :]
        buffers, semaphores, rest = rest[:m], rest[m], rest[m + 1 :]
        sources = [v if cols is None else v.at[:, pl.ds(cols[0], cols[1] - cols[0])] for v, cols in zip(sources, ranges)]
        staged = [Staged(source, buffer, semaphores.at[t]) for t, (source, buffer) in enumerate(zip(sources, buffers))]
        kernel(*first, *staged, *results, *rest)

    return pl.pallas_call(
        body,
        out_shape=outs,
        in_specs=[pl.BlockSpec(memory_space=pltpu.SMEM)] * n + [pl.BlockSpec(memory_space=pl.ANY)] * m,
        out_specs=tuple(pl.BlockSpec(memory_space=pltpu.VMEM) for _ in outs),
        scratch_shapes=[pltpu.VMEM(dims, v.dtype) for v, dims in zip(operands, shapes)] + [pltpu.SemaphoreType.DMA((m,))] + list(scratch),
        compiler_params=pltpu.CompilerParams(vmem_limit_bytes=vmem << 20),
        cost_estimate=pl.CostEstimate(flops=flops, bytes_accessed=1 << 22, transcendentals=0),
    )(*scalars, *operands)


def shape(*dims, dtype=F32):
    return jax.ShapeDtypeStruct(dims, dtype)


def cut_kernel(pattern, a, c, k, by_x, own_z, fold, cw, m1, m2):
    row = lax.axis_index("row")

    def block_a(i, q):
        return a[pl.ds(i * 512 + q, W, stride=4), :]

    def block_k(j, q):
        return k[pl.ds(j * 256 + q, W, stride=2), :]

    def lay(out, *blocks):
        for n, block in enumerate(blocks):
            out[:, n * W : (n + 1) * W] = block

    lay(by_x, block_k(0, 0), block_k(1, 0), block_a(1, 0), block_a(1, 1))
    lay(own_z, block_a(1, 3), block_k(1, 1), block_a(1, 2), block_a(0, 0))
    lay(fold, block_a(0, 1), block_k(0, 1))
    for j in range(2):
        for i in range(2):
            kept = pattern[j, row + 16 * i].astype(F32)
            for q in range(2):
                block = c[pl.ds((j * 2 + i) * 256 + q, W, stride=2), :]
                cw[pl.ds((j * 2 + i) * W, W), q * W : (q + 1) * W] = block * kept
    even = row % 2 == 0
    for m, (i, q) in enumerate(((0, 0), (1, 0), (1, 2))):
        low, high = block_a(i, q).T, block_a(i, q + 1).T
        m1[pl.ds(m * W, W), :] = jnp.where(even, low, high)
        m2[pl.ds(m * W, W), :] = jnp.where(even, high, low)


def block_of(pieces, b, cols):
    return pieces[b // 4][pl.ds((b % 4) * W, W), cols]


def fold_home(from_x, from_z):
    kind = (from_x >= 2).astype(jnp.int32)
    return kind, jnp.where(from_x < 2, 1 - from_x, from_x - 2) * 4 + from_z


def rows_kernel(cw, high, low):
    for column in range(8):
        for q in range(2):
            for j in range(2):
                here = (j, slice(None), slice((column + 8 * q) * W, (column + 8 * q + 1) * W))
                put(high, low, here, cw[column, pl.ds(j * 256, 256), q * W : (q + 1) * W])


def update_kernel(high, low, *refs):
    by_x, by_z = refs[:4], refs[4:8]
    (u0, u1), (rh, rl, eh, el) = refs[8:10], refs[10:]
    x, z, d = place()
    for b in range(16):
        row = origin(x, b % 4, d) * 4 + origin(z, b // 4, d)
        put(rh, rl, (at(row, W), slice(None)), block_of(by_x, b, slice(None)))
        kind, row = fold_home(origin(x, b // 4, d), origin(z, b % 4, d))
        put(eh, el, (kind, at(row, W), slice(None)), block_of(by_z, b, slice(None)))
    everything, upper = slice(None), slice(1024, 2048)
    for j in range(2):
        cols = slice(j * W, (j + 1) * W)
        first = dot3((high[j, :, everything], low[j, :, everything]), (rh[:, cols], rl[:, cols]))
        second = dot3((high[j, :, upper], low[j, :, upper]), (eh[j], el[j]))
        for i, u in enumerate((u0, u1)):
            u[:, 2 * j * W : (2 * j + 1) * W] = first[i * W : (i + 1) * W]
            u[:, (2 * j + 1) * W : (2 * j + 2) * W] = second[i * W : (i + 1) * W]


def root_kernel(m, *refs):
    by_x, by_z = refs[:4], refs[4:8]
    (s_out, root_out), (h0, l0, h1, l1, rh, rl, r0h, r0l, eh, el) = refs[8:10], refs[10:]
    x, z, d = place()
    upper = (4 * x + z >= 8).astype(jnp.int32)
    for column in range(8):
        for n in range(2):
            here = at(2 * column + (n + upper) % 2, W)
            for part, (hr, lr, lo) in enumerate(((h0, l0, 0), (h1, l1, 0), (h1, l1, W))):
                put(hr, lr, (pl.ds(lo, W), here), m[column, pl.ds((n * 3 + part) * W, W), :])
    for b in range(16):
        row = origin(x, b % 4, d) * 4 + origin(z, b // 4, d)
        put(rh, rl, (at(row, W), slice(0, 2 * W)), block_of(by_x, b, slice(None)))
        from_x, from_z = origin(x, b // 4, d), origin(z, b % 4, d)
        row = 4 * from_x + from_z
        put(rh, rl, (at(row, W), slice(2 * W, 3 * W)), block_of(by_z, b, slice(2 * W, 3 * W)))
        put(r0h, r0l, (at(row, W), slice(None)), block_of(by_z, b, slice(3 * W, 4 * W)))
        kind, row = fold_home(from_x, from_z)
        put(eh, el, (kind, at(row, W), slice(None)), block_of(by_z, b, slice(0, W)))
    late = slice(1024, 2048)
    s_out[:, : 3 * W] = dot3((h1[...], l1[...]), (rh[...], rl[...]))
    s_out[:, 3 * W :] = dot3((h1[:, late], l1[:, late]), (eh[1], el[1]))
    s_out[:W, :W] += dot3((h0[...], l0[...]), (r0h[...], r0l[...]))
    s_out[:W, W : 2 * W] += dot3((h0[:, late], l0[:, late]), (eh[0], el[0]))
    for i in range(2):
        for q in range(4):
            root_out[pl.ds(i * 512 + q, W, stride=4), :] = s_out[pl.ds(i * W, W), q * W : (q + 1) * W]


def halves_kernel(*refs):
    for n in range(6):
        put(refs[6], refs[7], (pl.ds(n * 512, 512), slice(None)), refs[n][...])


def product_kernel(pattern, s_in, early_high, early_low, *refs):
    late, (u0, u1, k), (p_out, *g_out), (high, low) = refs[:2], refs[2:5], refs[5:8], refs[8:]
    row = lax.axis_index("row")
    x, z, d = place()
    for column in range(8):
        for q in range(4):
            block = column + 8 * (q % 2)
            along_x, along_z = step_of(block // 4, x, d), step_of(block % 4, z, d)
            block = along_x + 4 * along_z if q < 2 else 16 + along_z + 4 * along_x
            put(high, low, (slice(None), at(block, W)), s_in[column, :, q * W : (q + 1) * W])
    total = jnp.zeros((256, 512), F32)
    for n in range(2):
        part, rows = slice(n * 2048, n * 2048 + 1536), slice(n * 1536, (n + 1) * 1536)
        total = total + dot3((high[:, part], low[:, part]), (early_high[rows, :], early_low[rows, :]))
        part = slice(n * 2048 + 1536, (n + 1) * 2048)
        total = total + dot3((high[:, part], low[:, part]), split(late[n][...]))
    for j in range(2):
        for q in range(2):
            cols = slice((2 * j + q) * W, (2 * j + q + 1) * W)
            own = k[pl.ds(j * 256 + q, W, stride=2), :]
            block = dot3(split(own.T), split(own))
            for i, u in enumerate((u0, u1)):
                scaled = total[i * W : (i + 1) * W, cols] * -pattern[j, row + 16 * i].astype(F32)
                p_out[pl.ds((j * 2 + i) * 256 + q, W, stride=2), :] = scaled
                block = block - dot3(split(u[:, cols].T), split(scaled))
            g_out[j][pl.ds(q, W, stride=2), :] = block


def local(root_inverse, child_coupling, child_inverse, pattern):
    a = root_inverse.reshape(1024, W)
    c = child_coupling.reshape(1024, W)
    k = child_inverse.reshape(512, W)
    by_x, own_z, fold, cw, m1, m2 = call(
        cut_kernel,
        (shape(W, 512), shape(W, 512), shape(W, 256), shape(512, 256), shape(384, W), shape(384, W)),
        (a, c, k),
        scalars=(pattern,),
    )

    folded = jnp.where(lax.axis_index("row") >= 8, own_z[:, : 2 * W], send(fold, FOLD))
    by_z = jnp.concatenate([folded, own_z[:, 2 * W :]], axis=1)
    m1, m2 = send(m1, MIRROR_1), send(m2, MIRROR_2)
    x_parts, z_parts, four = gather(by_x, by_z, m1, m2)
    mirrored = lax.all_gather(jnp.concatenate([after(m1, four), after(m2, four)], axis=0), "col")
    coupling = lax.all_gather(cw, "col")
    rows = call(rows_kernel, (shape(2, 256, 2048, dtype=BF16),) * 2, (coupling,), flops=1 << 20)
    u0, u1 = call(
        update_kernel,
        (shape(W, 512),) * 2,
        (*rows, *((v, (0, 256)) for v in x_parts), *((v, (128, 256)) for v in z_parts)),
        scratch=[pltpu.VMEM((2048, 256), BF16)] * 2 + [pltpu.VMEM((2, 1024, W), BF16)] * 2,
        flops=1 << 31,
    )

    first, second, begun = gather(u0, u1)
    sigma, sigma_root = call(
        root_kernel,
        (shape(256, 512), shape(1024, W)),
        (after(mirrored, begun), *((v, (256, 512)) for v in x_parts), *z_parts),
        scratch=[pltpu.VMEM((W, 2048), BF16)] * 2
        + [pltpu.VMEM((256, 2048), BF16)] * 2
        + [pltpu.VMEM((2048, 384), BF16)] * 2
        + [pltpu.VMEM((2048, W), BF16)] * 2
        + [pltpu.VMEM((2, 1024, W), BF16)] * 2,
        flops=1 << 31,
    )
    early = call(halves_kernel, (shape(3072, 512, dtype=BF16),) * 2, (*first[:3], *second[:3]), flops=1 << 36)
    p, g0, g1 = call(
        product_kernel,
        (shape(1024, W), shape(256, W), shape(256, W)),
        (lax.all_gather(sigma, "col"), *early, first[3], second[3], u0, u1, k),
        scalars=(pattern,),
        scratch=[pltpu.VMEM((256, 4096), BF16)] * 2,
        flops=1 << 30,
    )
    for along_x, along_z in zip(FLIP_X + FLIP_Z, FLIP_Z + FLIP_X):
        g0, g1 = g0 + send(g0, along_x), g1 + send(g1, along_z)
    g = jnp.concatenate([g0, g1], axis=0)
    return sigma_root.reshape(2, W, 4, W), p.reshape(2, 2, W, 2, W), g.reshape(2, W, 2, W)


def solution(mesh):
    in_specs = (
        P(None, "row", None, "col"),
        P(None, None, "row", None, "col"),
        P(None, None, "row", None, "col"),
        P(),
    )
    out_specs = (
        P(None, "row", None, "col"),
        P(None, None, "row", None, "col"),
        P(None, None, None, "col"),
    )
    return jax.shard_map(local, mesh=mesh, in_specs=in_specs, out_specs=out_specs, check_vma=False)
```

```python
import functools

import jax
import jax.numpy as jnp
from jax import lax
from jax.experimental import pallas as pl
from jax.experimental.pallas import tpu as pltpu
from jax.sharding import PartitionSpec as P

X, Z, Y, CORES = 4, 4, 4, 2
W = 128
F32, BF16 = jnp.float32, jnp.bfloat16
AXES = ("row", "col")


def moves(target):
    pairs = []
    for x in range(X):
        for z in range(Z):
            for y in range(Y):
                for core in range(CORES):
                    there = target(x, z, y, core)
                    if there is not None:
                        u, w, v, k = there
                        pairs.append((((x * Z + z) * Y + y) * CORES + core, ((u * Z + w) * Y + v) * CORES + k))
    return pairs


FLIPS = ((1, 3), (3, 1))
ALONG_X = [moves(lambda x, z, y, k, n=n: (x ^ FLIPS[k][n], z, y, k)) for n in range(2)]
ALONG_Z = [moves(lambda x, z, y, k, n=n: (x, z ^ FLIPS[k][n], y, k)) for n in range(2)]
ALONG_Y = [moves(lambda x, z, y, k, n=n: (x, z, y ^ FLIPS[k][n], k)) for n in range(2)]
SWAP = moves(lambda x, z, y, k: (x, z, y, 1 - k))
FOLD = moves(lambda x, z, y, k: (3 - x, z, y, k) if x >= 2 else None)


def mirror(first):
    def target(x, z, y, k):
        r, c = x * Z + z, y * CORES + k
        to = c if (r % 2 == 0) == first else c + 8
        return to // Z, to % Z, (r // 2) // CORES, (r // 2) % CORES

    return moves(target)


MIRROR_1, MIRROR_2 = mirror(True), mirror(False)


def send(value, pairs):
    return lax.ppermute(value, AXES, pairs)


def both(value, pairs):
    return jnp.concatenate([value, send(value, pairs)], axis=0)


def after(value, *others):
    return lax.optimization_barrier((value, *others))[0]


def gather(value, first, second):
    eight = both(both(both(value, first[0]), first[1]), second[0])
    return [eight, send(eight, second[1])]


def share(value):
    four = both(both(value, ALONG_Y[0]), ALONG_Y[1])
    return [four, send(four, SWAP)]


def place():
    row, col = lax.axis_index("row"), lax.axis_index("col")
    return row // 4, row % 4, col // 2, col % 2


def origin(index, step, core):
    if step == 0:
        return index
    if step == 3:
        return index ^ 2
    return index ^ jnp.where(core == step - 1, 1, 3)


def step_of(there, here, core):
    flip = there ^ here
    swapped = jnp.where(flip == 0, 0, jnp.where(flip == 2, 3, jnp.where(flip == 1, 1, 2)))
    return jnp.where((core == 1) & ((flip == 1) | (flip == 3)), 3 - swapped, swapped)


def column_of(w, y, core):
    owner = core if w < 4 else 1 - core
    return 2 * origin(y, w % 4, owner) + owner


def at(index, size):
    return pl.ds(pl.multiple_of(index * size, size), size)


def split(value):
    high = value.astype(BF16)
    return high, (value - high.astype(F32)).astype(BF16)


def put(high, low, where, value):
    h, l = split(value)
    high[where] = h
    low[where] = l


def dot3(left, right):
    dot = functools.partial(jnp.dot, preferred_element_type=F32)
    return dot(left[0], right[0]) + (dot(left[0], right[1]) + dot(left[1], right[0]))


def call(kernel, outs, scratch=(), smem_first=False, count=0, flops=0, vmem=24):
    in_specs = [pl.BlockSpec(memory_space=pltpu.VMEM)] * count
    if smem_first:
        in_specs = [pl.BlockSpec(memory_space=pltpu.SMEM)] + in_specs
    return pl.pallas_call(
        kernel,
        out_shape=outs,
        in_specs=in_specs,
        out_specs=jax.tree.map(lambda _: pl.BlockSpec(memory_space=pltpu.VMEM), outs),
        scratch_shapes=list(scratch),
        compiler_params=pltpu.CompilerParams(vmem_limit_bytes=vmem << 20),
        cost_estimate=pl.CostEstimate(flops=flops, bytes_accessed=1 << 22, transcendentals=0),
    )


def shape(*dims, dtype=F32):
    return jax.ShapeDtypeStruct(dims, dtype)


def cut_kernel(pattern, a, c, k, k_main, fold, keep_own, ax, az, cw, m1, m2):
    row = lax.axis_index("row")

    def block_a(i, q):
        return a[pl.ds(i * 512 + q, W, stride=4), :]

    def block_k(j, q):
        return k[pl.ds(j * 256 + q, W, stride=2), :]

    left, right = slice(0, W), slice(W, 2 * W)
    k_main[:, left] = block_k(0, 0)
    k_main[:, right] = block_k(1, 0)
    fold[:, left] = block_a(0, 1)
    fold[:, right] = block_k(0, 1)
    keep_own[:, left] = block_a(1, 3)
    keep_own[:, right] = block_k(1, 1)
    ax[:, left] = block_a(1, 0)
    ax[:, right] = block_a(1, 1)
    az[:, left] = block_a(1, 2)
    az[:, right] = block_a(0, 0)
    for j in range(2):
        for i in range(2):
            kept = pattern[j, row + 16 * i].astype(F32)
            for q in range(2):
                block = c[pl.ds((j * 2 + i) * 256 + q, W, stride=2), :]
                cw[pl.ds((j * 2 + i) * W, W), q * W : (q + 1) * W] = block * kept
    even = row % 2 == 0
    for m, (i, q) in enumerate(((0, 0), (1, 0), (1, 2))):
        low, high = block_a(i, q).T, block_a(i, q + 1).T
        m1[pl.ds(m * W, W), :] = jnp.where(even, low, high)
        m2[pl.ds(m * W, W), :] = jnp.where(even, high, low)


def block_of(pieces, b):
    return pieces[b // 8][pl.ds((b % 8) * W, W), :]


def fold_home(b, x, z, core):
    from_z, from_x = origin(z, b % 4, core), origin(x, b // 4, core)
    kind = (from_x >= 2).astype(jnp.int32)
    return kind, jnp.where(from_x < 2, 1 - from_x, from_x - 2) * 4 + from_z


def update_kernel(*refs):
    cw, main, fold = refs[:2], refs[2:4], refs[4:6]
    outs, (high, low, rh, rl, eh, el) = refs[6:10], refs[10:]
    x, z, y, core = place()
    for w in range(8):
        column = column_of(w, y, core)
        for q in range(2):
            for j in range(2):
                block = cw[w // 4][pl.ds((w % 4) * 512 + j * 256, 256), q * W : (q + 1) * W]
                put(high, low, (j, slice(None), at(column + 8 * q, W)), block)
    for b in range(16):
        row = origin(x, b % 4, core) * 4 + origin(z, b // 4, core)
        put(rh, rl, (at(row, W), slice(None)), block_of(main, b))
        kind, row = fold_home(b, x, z, core)
        put(eh, el, (kind, at(row, W), slice(None)), block_of(fold, b)[:, W:])
    for j in range(2):
        cols = slice(j * W, (j + 1) * W)
        first = dot3((high[j], low[j]), (rh[:, cols], rl[:, cols]))
        upper = slice(1024, 2048)
        second = dot3((high[j, :, upper], low[j, :, upper]), (eh[j], el[j]))
        for i in range(2):
            outs[2 * j + i][:, :W] = first[i * W : (i + 1) * W]
            outs[2 * j + i][:, W:] = second[i * W : (i + 1) * W]


def root_kernel(*refs):
    m, ax, az, fold = refs[:2], refs[2:4], refs[4:6], refs[6:8]
    (s_out, root_out), (h0, l0, h1, l1, rh, rl, r0h, r0l, eh, el) = refs[8:10], refs[10:]
    x, z, y, core = place()
    upper = (4 * x + z >= 8).astype(jnp.int32)
    for w in range(8):
        column = column_of(w, y, core)
        for n in range(2):
            here = at(2 * column + (n + upper) % 2, W)
            for part, (hr, lr, lo) in enumerate(((h0, l0, 0), (h1, l1, 0), (h1, l1, W))):
                block = m[w // 4][pl.ds(((w % 4) * 6 + n * 3 + part) * W, W), :]
                put(hr, lr, (pl.ds(lo, W), here), block)
    for b in range(16):
        row = origin(x, b % 4, core) * 4 + origin(z, b // 4, core)
        put(rh, rl, (at(row, W), slice(0, 2 * W)), block_of(ax, b))
        row = origin(z, b % 4, core) + origin(x, b // 4, core) * 4
        block = block_of(az, b)
        put(rh, rl, (at(row, W), slice(2 * W, 3 * W)), block[:, :W])
        put(r0h, r0l, (at(row, W), slice(None)), block[:, W:])
        kind, row = fold_home(b, x, z, core)
        put(eh, el, (kind, at(row, W), slice(None)), block_of(fold, b)[:, :W])
    late = slice(1024, 2048)
    s_out[:, : 3 * W] = dot3((h1[...], l1[...]), (rh[...], rl[...]))
    s_out[:, 3 * W :] = dot3((h1[:, late], l1[:, late]), (eh[1], el[1]))
    s_out[:W, :W] += dot3((h0[...], l0[...]), (r0h[...], r0l[...]))
    s_out[:W, W : 2 * W] += dot3((h0[:, late], l0[:, late]), (eh[0], el[0]))
    for i in range(2):
        for q in range(4):
            root_out[pl.ds(i * 512 + q, W, stride=4), :] = s_out[pl.ds(i * W, W), q * W : (q + 1) * W]


def order_kernel(*refs):
    s_in, (high, low) = refs[:2], refs[2:]
    x, z, y, core = place()
    for w in range(8):
        column = column_of(w, y, core)
        for q in range(4):
            row = column + 8 * (q % 2)
            along_x, along_z = step_of(row // 4, x, core), step_of(row % 4, z, core)
            block = along_x + 4 * along_z if q < 2 else 16 + along_z + 4 * along_x
            put(high, low, (slice(None), at(block, W)), s_in[w // 4][pl.ds((w % 4) * 256, 256), q * W : (q + 1) * W])


def early_kernel(high, low, p0, p1, total):
    first = dot3((high[:, :1024], low[:, :1024]), split(p0[...]))
    total[...] = first + dot3((high[:, 2048:3072], low[:, 2048:3072]), split(p1[...]))


def product_kernel(j, pattern, high, low, early, p0, p1, u0, u1, k, p_out, g_out):
    row = lax.axis_index("row")
    total = early[...] + dot3((high[:, 1024:2048], low[:, 1024:2048]), split(p0[...]))
    total = total + dot3((high[:, 3072:], low[:, 3072:]), split(p1[...]))
    scaled = [total[i * W : (i + 1) * W] * -pattern[j, row + 16 * i].astype(F32) for i in range(2)]
    for q in range(2):
        cols = slice(q * W, (q + 1) * W)
        own = k[pl.ds(j * 256 + q, W, stride=2), :]
        block = dot3(split(own.T), split(own))
        for i, u in enumerate((u0, u1)):
            p_out[pl.ds(i * 256 + q, W, stride=2), :] = scaled[i][:, cols]
            block = block - dot3(split(u[:, cols].T), split(scaled[i][:, cols]))
        g_out[pl.ds(q, W, stride=2), :] = block


def local(root_inverse, child_coupling, child_inverse, pattern):
    a = root_inverse.reshape(1024, W)
    c = child_coupling.reshape(1024, W)
    k = child_inverse.reshape(512, W)
    k_main, fold, keep_own, ax, az, cw, m1, m2 = call(
        cut_kernel,
        (shape(W, 256),) * 5 + (shape(512, 256), shape(384, W), shape(384, W)),
        smem_first=True,
        count=3,
    )(pattern, a, c, k)

    folded = jnp.where(lax.axis_index("row") >= 8, keep_own, send(fold, FOLD))
    main_parts = gather(k_main, ALONG_X, ALONG_Z)
    fold_parts = gather(folded, ALONG_Z, ALONG_X)
    coupling_parts = share(cw)
    u = call(
        update_kernel,
        (shape(W, 256),) * 4,
        scratch=[pltpu.VMEM((2, 256, 2048), BF16)] * 2 + [pltpu.VMEM((2048, 256), BF16)] * 2 + [pltpu.VMEM((2, 1024, W), BF16)] * 2,
        count=6,
        flops=1 << 31,
    )(*coupling_parts, *main_parts, *fold_parts)

    ax_parts = gather(ax, ALONG_X, ALONG_Z)
    az_parts = gather(az, ALONG_Z, ALONG_X)
    mirrored = share(jnp.concatenate([send(m1, MIRROR_1), send(m2, MIRROR_2)], axis=0))
    sigma, sigma_root = call(
        root_kernel,
        (shape(256, 512), shape(1024, W)),
        scratch=[pltpu.VMEM((W, 2048), BF16)] * 2
        + [pltpu.VMEM((256, 2048), BF16)] * 2
        + [pltpu.VMEM((2048, 384), BF16)] * 2
        + [pltpu.VMEM((2048, W), BF16)] * 2
        + [pltpu.VMEM((2, 1024, W), BF16)] * 2,
        count=8,
        flops=1 << 31,
    )(after(mirrored[0], u[0]), mirrored[1], *ax_parts, *az_parts, *fold_parts)
    high, low = call(order_kernel, (shape(256, 4096, dtype=BF16),) * 2, count=2, flops=1 << 20)(*share(sigma))

    products, diagonals = [], []
    for j in range(2):
        u0, u1 = u[2 * j], u[2 * j + 1]
        first, second = gather(u0, ALONG_X, ALONG_Z), gather(u1, ALONG_Z, ALONG_X)
        early = call(early_kernel, shape(256, 256), count=4, flops=1 << 30)(high, low, first[0], second[0])
        p, g = call(
            functools.partial(product_kernel, j),
            (shape(512, W), shape(256, W)),
            smem_first=True,
            count=8,
            flops=1 << 30,
        )(pattern, high, low, early, first[1], second[1], u0, u1, k)
        for pairs in ALONG_X + ALONG_Z:
            g = g + send(g, pairs)
        diagonals.append(g)
        products.append(p)
    return (
        sigma_root.reshape(2, W, 4, W),
        jnp.concatenate(products).reshape(2, 2, W, 2, W),
        jnp.concatenate(diagonals).reshape(2, W, 2, W),
    )


def solution(mesh):
    in_specs = (
        P(None, "row", None, "col"),
        P(None, None, "row", None, "col"),
        P(None, None, "row", None, "col"),
        P(),
    )
    out_specs = (
        P(None, "row", None, "col"),
        P(None, None, "row", None, "col"),
        P(None, None, None, "col"),
    )
    return jax.shard_map(local, mesh=mesh, in_specs=in_specs, out_specs=out_specs, check_vma=False)
```

```python
import functools

import jax
import jax.numpy as jnp
from jax import lax
from jax.experimental import pallas as pl
from jax.experimental.pallas import tpu as pltpu
from jax.sharding import PartitionSpec as P

X, Z, Y, CORES = 4, 4, 4, 2
W = 128
HINT = 1 << 36
F32, BF16 = jnp.float32, jnp.bfloat16
AXES = ("row", "col")


def moves(target):
    pairs = []
    for x in range(X):
        for z in range(Z):
            for y in range(Y):
                for core in range(CORES):
                    there = target(x, z, y, core)
                    if there is not None:
                        u, w, v, k = there
                        pairs.append((((x * Z + z) * Y + y) * CORES + core, ((u * Z + w) * Y + v) * CORES + k))
    return pairs


FLIPS = ((1, 3), (3, 1))
ALONG_X = [moves(lambda x, z, y, k, n=n: (x ^ FLIPS[k][n], z, y, k)) for n in range(2)]
ALONG_Z = [moves(lambda x, z, y, k, n=n: (x, z ^ FLIPS[k][n], y, k)) for n in range(2)]
ALONG_Y = [moves(lambda x, z, y, k, n=n: (x, z, y ^ FLIPS[k][n], k)) for n in range(2)]
SWAP = moves(lambda x, z, y, k: (x, z, y, 1 - k))
FOLD = moves(lambda x, z, y, k: (3 - x, z, y, k) if x >= 2 else None)


def mirror(first):
    def target(x, z, y, k):
        r, c = x * Z + z, y * CORES + k
        to = c if (r % 2 == 0) == first else c + 8
        return to // Z, to % Z, (r // 2) // CORES, (r // 2) % CORES

    return moves(target)


MIRROR_1, MIRROR_2 = mirror(True), mirror(False)


def send(value, pairs):
    return lax.ppermute(value, AXES, pairs)


def both(value, pairs):
    return jnp.concatenate([value, send(value, pairs)], axis=0)


def after(value, *others):
    return lax.optimization_barrier((value, *others))[0]


def gather(value, first, second):
    two = both(value, first[0])
    eight = both(both(two, first[1]), second[0])
    return [eight, send(eight, second[1])], two


def share(value):
    four = both(both(value, ALONG_Y[0]), ALONG_Y[1])
    return [four, send(four, SWAP)]


def place():
    row, col = lax.axis_index("row"), lax.axis_index("col")
    return row // 4, row % 4, col // 2, col % 2


def origin(index, step, core):
    if step == 0:
        return index
    if step == 3:
        return index ^ 2
    return index ^ jnp.where(core == step - 1, 1, 3)


def step_of(there, here, core):
    flip = there ^ here
    swapped = jnp.where(flip == 0, 0, jnp.where(flip == 2, 3, jnp.where(flip == 1, 1, 2)))
    return jnp.where((core == 1) & ((flip == 1) | (flip == 3)), 3 - swapped, swapped)


def column_of(w, y, core):
    owner = core if w < 4 else 1 - core
    return 2 * origin(y, w % 4, owner) + owner


def at(index, size):
    return pl.ds(pl.multiple_of(index * size, size), size)


def split(value):
    high = value.astype(BF16)
    return high, (value - high.astype(F32)).astype(BF16)


def put(high, low, where, value):
    h, l = split(value)
    high[where] = h
    low[where] = l


def dot3(left, right):
    dot = functools.partial(jnp.dot, preferred_element_type=F32)
    return dot(left[0], right[0]) + (dot(left[0], right[1]) + dot(left[1], right[0]))


def call(kernel, outs, scratch=(), smem_first=False, count=0, flops=0, vmem=24):
    in_specs = [pl.BlockSpec(memory_space=pltpu.VMEM)] * count
    if smem_first:
        in_specs = [pl.BlockSpec(memory_space=pltpu.SMEM)] + in_specs
    return pl.pallas_call(
        kernel,
        out_shape=outs,
        in_specs=in_specs,
        out_specs=jax.tree.map(lambda _: pl.BlockSpec(memory_space=pltpu.VMEM), outs),
        scratch_shapes=list(scratch),
        compiler_params=pltpu.CompilerParams(vmem_limit_bytes=vmem << 20),
        cost_estimate=pl.CostEstimate(flops=flops, bytes_accessed=1 << 22, transcendentals=0),
    )


class Staged:
    def __init__(self, source, buffer, semaphore):
        self.copy, self.buffer, self.shape, self.here = pltpu.make_async_copy(source, buffer, semaphore), buffer, buffer.shape, False
        self.copy.start()

    def __getitem__(self, where):
        if not self.here:
            self.copy.wait()
            self.here = True
        return self.buffer[where]


def staged_call(kernel, outs, operands, scratch=(), scalars=(), flops=0, vmem=56):
    operands = [v if isinstance(v, tuple) else (v, None) for v in operands]
    ranges, operands = [v[1] for v in operands], [v[0] for v in operands]
    shapes = [v.shape if cols is None else (v.shape[0], cols[1] - cols[0]) for v, cols in zip(operands, ranges)]
    n, m = len(scalars), len(operands)

    def body(*refs):
        first, sources, rest = refs[:n], refs[n : n + m], refs[n + m :]
        results, rest = rest[: len(outs)], rest[len(outs) :]
        buffers, semaphores, rest = rest[:m], rest[m], rest[m + 1 :]
        sources = [v if cols is None else v.at[:, pl.ds(cols[0], cols[1] - cols[0])] for v, cols in zip(sources, ranges)]
        staged = [Staged(source, buffer, semaphores.at[t]) for t, (source, buffer) in enumerate(zip(sources, buffers))]
        kernel(*first, *staged, *results, *rest)

    return pl.pallas_call(
        body,
        out_shape=outs,
        in_specs=[pl.BlockSpec(memory_space=pltpu.SMEM)] * n + [pl.BlockSpec(memory_space=pl.ANY)] * m,
        out_specs=tuple(pl.BlockSpec(memory_space=pltpu.VMEM) for _ in outs),
        scratch_shapes=[pltpu.VMEM(dims, v.dtype) for v, dims in zip(operands, shapes)] + [pltpu.SemaphoreType.DMA((m,))] + list(scratch),
        compiler_params=pltpu.CompilerParams(vmem_limit_bytes=vmem << 20),
        cost_estimate=pl.CostEstimate(flops=flops, bytes_accessed=1 << 22, transcendentals=0),
    )(*scalars, *operands)


def shape(*dims, dtype=F32):
    return jax.ShapeDtypeStruct(dims, dtype)


def cut_kernel(pattern, a, c, k, k_main, fold, keep_own, ax, az, cw, m1, m2):
    row = lax.axis_index("row")

    def block_a(i, q):
        return a[pl.ds(i * 512 + q, W, stride=4), :]

    def block_k(j, q):
        return k[pl.ds(j * 256 + q, W, stride=2), :]

    left, right = slice(0, W), slice(W, 2 * W)
    k_main[:, left] = block_k(0, 0)
    k_main[:, right] = block_k(1, 0)
    fold[:, left] = block_a(0, 1)
    fold[:, right] = block_k(0, 1)
    keep_own[:, left] = block_a(1, 3)
    keep_own[:, right] = block_k(1, 1)
    ax[:, left] = block_a(1, 0)
    ax[:, right] = block_a(1, 1)
    az[:, left] = block_a(1, 2)
    az[:, right] = block_a(0, 0)
    for j in range(2):
        for i in range(2):
            kept = pattern[j, row + 16 * i].astype(F32)
            for q in range(2):
                block = c[pl.ds((j * 2 + i) * 256 + q, W, stride=2), :]
                cw[pl.ds((j * 2 + i) * W, W), q * W : (q + 1) * W] = block * kept
    even = row % 2 == 0
    for m, (i, q) in enumerate(((0, 0), (1, 0), (1, 2))):
        low, high = block_a(i, q).T, block_a(i, q + 1).T
        m1[pl.ds(m * W, W), :] = jnp.where(even, low, high)
        m2[pl.ds(m * W, W), :] = jnp.where(even, high, low)


def block_of(pieces, b):
    return pieces[b // 8][pl.ds((b % 8) * W, W), :]


def fold_home(b, x, z, core):
    from_z, from_x = origin(z, b % 4, core), origin(x, b // 4, core)
    kind = (from_x >= 2).astype(jnp.int32)
    return kind, jnp.where(from_x < 2, 1 - from_x, from_x - 2) * 4 + from_z


def update_kernel(*refs):
    cw, main, fold = refs[:2], refs[2:4], refs[4:6]
    outs, (high, low, rh, rl, eh, el) = refs[6:10], refs[10:]
    x, z, y, core = place()
    for w in range(8):
        column = column_of(w, y, core)
        for q in range(2):
            for j in range(2):
                block = cw[w // 4][pl.ds((w % 4) * 512 + j * 256, 256), q * W : (q + 1) * W]
                put(high, low, (j, slice(None), at(column + 8 * q, W)), block)
    for b in range(16):
        row = origin(x, b % 4, core) * 4 + origin(z, b // 4, core)
        put(rh, rl, (at(row, W), slice(None)), block_of(main, b))
        kind, row = fold_home(b, x, z, core)
        put(eh, el, (kind, at(row, W), slice(None)), block_of(fold, b)[:, W:])
    for j in range(2):
        cols = slice(j * W, (j + 1) * W)
        first = dot3((high[j], low[j]), (rh[:, cols], rl[:, cols]))
        upper = slice(1024, 2048)
        second = dot3((high[j, :, upper], low[j, :, upper]), (eh[j], el[j]))
        for i in range(2):
            outs[2 * j + i][:, :W] = first[i * W : (i + 1) * W]
            outs[2 * j + i][:, W:] = second[i * W : (i + 1) * W]


def root_kernel(*refs):
    m, ax, az, fold = refs[:2], refs[2:4], refs[4:6], refs[6:8]
    (s_out, root_out), (h0, l0, h1, l1, rh, rl, r0h, r0l, eh, el) = refs[8:10], refs[10:]
    x, z, y, core = place()
    upper = (4 * x + z >= 8).astype(jnp.int32)
    for w in range(8):
        column = column_of(w, y, core)
        for n in range(2):
            here = at(2 * column + (n + upper) % 2, W)
            for part, (hr, lr, lo) in enumerate(((h0, l0, 0), (h1, l1, 0), (h1, l1, W))):
                block = m[w // 4][pl.ds(((w % 4) * 6 + n * 3 + part) * W, W), :]
                put(hr, lr, (pl.ds(lo, W), here), block)
    for b in range(16):
        row = origin(x, b % 4, core) * 4 + origin(z, b // 4, core)
        put(rh, rl, (at(row, W), slice(0, 2 * W)), block_of(ax, b))
        row = origin(z, b % 4, core) + origin(x, b // 4, core) * 4
        block = block_of(az, b)
        put(rh, rl, (at(row, W), slice(2 * W, 3 * W)), block[:, :W])
        put(r0h, r0l, (at(row, W), slice(None)), block[:, W:])
        kind, row = fold_home(b, x, z, core)
        put(eh, el, (kind, at(row, W), slice(None)), block_of(fold, b)[:, :W])
    late = slice(1024, 2048)
    s_out[:, : 3 * W] = dot3((h1[...], l1[...]), (rh[...], rl[...]))
    s_out[:, 3 * W :] = dot3((h1[:, late], l1[:, late]), (eh[1], el[1]))
    s_out[:W, :W] += dot3((h0[...], l0[...]), (r0h[...], r0l[...]))
    s_out[:W, W : 2 * W] += dot3((h0[:, late], l0[:, late]), (eh[0], el[0]))
    for i in range(2):
        for q in range(4):
            root_out[pl.ds(i * 512 + q, W, stride=4), :] = s_out[pl.ds(i * W, W), q * W : (q + 1) * W]


def order_kernel(*refs):
    s_in, (high, low) = refs[:2], refs[2:]
    x, z, y, core = place()
    for w in range(8):
        column = column_of(w, y, core)
        for q in range(4):
            row = column + 8 * (q % 2)
            along_x, along_z = step_of(row // 4, x, core), step_of(row % 4, z, core)
            block = along_x + 4 * along_z if q < 2 else 16 + along_z + 4 * along_x
            put(high, low, (slice(None), at(block, W)), s_in[w // 4][pl.ds((w % 4) * 256, 256), q * W : (q + 1) * W])


def halves_kernel(a, b, high, low):
    put(high, low, (slice(0, 1024), slice(None)), a[...])
    put(high, low, (slice(1024, 2048), slice(None)), b[...])


def early_kernel(high, low, near_high, near_low, total):
    first = dot3((high[:, :1024], low[:, :1024]), (near_high[:1024, :], near_low[:1024, :]))
    total[...] = first + dot3((high[:, 2048:3072], low[:, 2048:3072]), (near_high[1024:, :], near_low[1024:, :]))


def product_kernel(j, pattern, high, low, early, p0, p1, u0, u1, k, p_out, g_out):
    row = lax.axis_index("row")
    total = early[...] + dot3((high[:, 1024:2048], low[:, 1024:2048]), split(p0[...]))
    total = total + dot3((high[:, 3072:], low[:, 3072:]), split(p1[...]))
    scaled = [total[i * W : (i + 1) * W] * -pattern[j, row + 16 * i].astype(F32) for i in range(2)]
    for q in range(2):
        cols = slice(q * W, (q + 1) * W)
        own = k[pl.ds(j * 256 + q, W, stride=2), :]
        block = dot3(split(own.T), split(own))
        for i, u in enumerate((u0, u1)):
            p_out[pl.ds(i * 256 + q, W, stride=2), :] = scaled[i][:, cols]
            block = block - dot3(split(u[:, cols].T), split(scaled[i][:, cols]))
        g_out[pl.ds(q, W, stride=2), :] = block


def local(root_inverse, child_coupling, child_inverse, pattern):
    a = root_inverse.reshape(1024, W)
    c = child_coupling.reshape(1024, W)
    k = child_inverse.reshape(512, W)
    k_main, fold, keep_own, ax, az, cw, m1, m2 = staged_call(
        cut_kernel,
        (shape(W, 256),) * 5 + (shape(512, 256), shape(384, W), shape(384, W)),
        (a, c, k),
        scalars=(pattern,),
    )

    folded = jnp.where(lax.axis_index("row") >= 8, keep_own, send(fold, FOLD))
    main_parts, _ = gather(k_main, ALONG_X, ALONG_Z)
    fold_parts, _ = gather(folded, ALONG_Z, ALONG_X)
    coupling_parts = share(cw)
    u = call(
        update_kernel,
        (shape(W, 256),) * 4,
        scratch=[pltpu.VMEM((2, 256, 2048), BF16)] * 2 + [pltpu.VMEM((2048, 256), BF16)] * 2 + [pltpu.VMEM((2, 1024, W), BF16)] * 2,
        count=6,
        flops=1 << 31,
    )(*coupling_parts, *main_parts, *fold_parts)

    ax_parts, _ = gather(ax, ALONG_X, ALONG_Z)
    az_parts, _ = gather(az, ALONG_Z, ALONG_X)
    mirrored = share(jnp.concatenate([send(m1, MIRROR_1), send(m2, MIRROR_2)], axis=0))
    panels, begun = [], []
    for j in range(2):
        (first, x_two), (second, z_two) = gather(u[2 * j], ALONG_X, ALONG_Z), gather(u[2 * j + 1], ALONG_Z, ALONG_X)
        panels.append((first, second))
        begun += [x_two, z_two]
    sigma, sigma_root = call(
        root_kernel,
        (shape(256, 512), shape(1024, W)),
        scratch=[pltpu.VMEM((W, 2048), BF16)] * 2
        + [pltpu.VMEM((256, 2048), BF16)] * 2
        + [pltpu.VMEM((2048, 384), BF16)] * 2
        + [pltpu.VMEM((2048, W), BF16)] * 2
        + [pltpu.VMEM((2, 1024, W), BF16)] * 2,
        count=8,
        flops=1 << 31,
    )(after(mirrored[0], *begun[:2]), mirrored[1], *ax_parts, *az_parts, *fold_parts)
    high, low = call(order_kernel, (shape(256, 4096, dtype=BF16),) * 2, count=2, flops=1 << 20)(*share(sigma))

    products, diagonals = [], []
    for j in range(2):
        u0, u1 = u[2 * j], u[2 * j + 1]
        first, second = panels[j]
        near = call(halves_kernel, (shape(2048, 256, dtype=BF16),) * 2, count=2, flops=HINT)(first[0], second[0])
        early = call(early_kernel, shape(256, 256), count=4, flops=1 << 30)(high, low, *near)
        p, g = call(
            functools.partial(product_kernel, j),
            (shape(512, W), shape(256, W)),
            smem_first=True,
            count=8,
            flops=1 << 30,
        )(pattern, high, low, early, first[1], second[1], u0, u1, k)
        for pairs in ALONG_X + ALONG_Z:
            g = g + send(g, pairs)
        diagonals.append(g)
        products.append(p)
    return (
        sigma_root.reshape(2, W, 4, W),
        jnp.concatenate(products).reshape(2, 2, W, 2, W),
        jnp.concatenate(diagonals).reshape(2, W, 2, W),
    )


def solution(mesh):
    in_specs = (
        P(None, "row", None, "col"),
        P(None, None, "row", None, "col"),
        P(None, None, "row", None, "col"),
        P(),
    )
    out_specs = (
        P(None, "row", None, "col"),
        P(None, None, "row", None, "col"),
        P(None, None, None, "col"),
    )
    return jax.shard_map(local, mesh=mesh, in_specs=in_specs, out_specs=out_specs, check_vma=False)
```

```python
import functools

import jax
import jax.numpy as jnp
from jax import lax
from jax.experimental import pallas as pl
from jax.experimental.pallas import tpu as pltpu
from jax.sharding import PartitionSpec as P

X, Z, Y, CORES = 4, 4, 4, 2
W = 128
HINT = 1 << 36
F32, BF16 = jnp.float32, jnp.bfloat16
AXES = ("row", "col")


def moves(target):
    pairs = []
    for x in range(X):
        for z in range(Z):
            for y in range(Y):
                for core in range(CORES):
                    there = target(x, z, y, core)
                    if there is not None:
                        u, w, v, k = there
                        pairs.append((((x * Z + z) * Y + y) * CORES + core, ((u * Z + w) * Y + v) * CORES + k))
    return pairs


FLIPS = ((1, 3), (3, 1))
ALONG_X = [moves(lambda x, z, y, k, n=n: (x ^ FLIPS[k][n], z, y, k)) for n in range(2)]
ALONG_Z = [moves(lambda x, z, y, k, n=n: (x, z ^ FLIPS[k][n], y, k)) for n in range(2)]
ALONG_Y = [moves(lambda x, z, y, k, n=n: (x, z, y ^ FLIPS[k][n], k)) for n in range(2)]
SWAP = moves(lambda x, z, y, k: (x, z, y, 1 - k))
FOLD = moves(lambda x, z, y, k: (3 - x, z, y, k) if x >= 2 else None)


def mirror(first):
    def target(x, z, y, k):
        r, c = x * Z + z, y * CORES + k
        to = c if (r % 2 == 0) == first else c + 8
        return to // Z, to % Z, (r // 2) // CORES, (r // 2) % CORES

    return moves(target)


MIRROR_1, MIRROR_2 = mirror(True), mirror(False)


def send(value, pairs):
    return lax.ppermute(value, AXES, pairs)


def both(value, pairs):
    return jnp.concatenate([value, send(value, pairs)], axis=0)


def after(value, *others):
    return lax.optimization_barrier((value, *others))[0]


def gather(value, first, second):
    two = both(value, first[0])
    eight = both(both(two, first[1]), second[0])
    return [eight, send(eight, second[1])], two


def share(value):
    four = both(both(value, ALONG_Y[0]), ALONG_Y[1])
    return [four, send(four, SWAP)]


def place():
    row, col = lax.axis_index("row"), lax.axis_index("col")
    return row // 4, row % 4, col // 2, col % 2


def origin(index, step, core):
    if step == 0:
        return index
    if step == 3:
        return index ^ 2
    return index ^ jnp.where(core == step - 1, 1, 3)


def step_of(there, here, core):
    flip = there ^ here
    swapped = jnp.where(flip == 0, 0, jnp.where(flip == 2, 3, jnp.where(flip == 1, 1, 2)))
    return jnp.where((core == 1) & ((flip == 1) | (flip == 3)), 3 - swapped, swapped)


def column_of(w, y, core):
    owner = core if w < 4 else 1 - core
    return 2 * origin(y, w % 4, owner) + owner


def at(index, size):
    return pl.ds(pl.multiple_of(index * size, size), size)


def split(value):
    high = value.astype(BF16)
    return high, (value - high.astype(F32)).astype(BF16)


def put(high, low, where, value):
    h, l = split(value)
    high[where] = h
    low[where] = l


def dot3(left, right):
    dot = functools.partial(jnp.dot, preferred_element_type=F32)
    return dot(left[0], right[0]) + (dot(left[0], right[1]) + dot(left[1], right[0]))


def call(kernel, outs, scratch=(), smem_first=False, count=0, flops=0, vmem=24):
    in_specs = [pl.BlockSpec(memory_space=pltpu.VMEM)] * count
    if smem_first:
        in_specs = [pl.BlockSpec(memory_space=pltpu.SMEM)] + in_specs
    return pl.pallas_call(
        kernel,
        out_shape=outs,
        in_specs=in_specs,
        out_specs=jax.tree.map(lambda _: pl.BlockSpec(memory_space=pltpu.VMEM), outs),
        scratch_shapes=list(scratch),
        compiler_params=pltpu.CompilerParams(vmem_limit_bytes=vmem << 20),
        cost_estimate=pl.CostEstimate(flops=flops, bytes_accessed=1 << 22, transcendentals=0),
    )


class Staged:
    def __init__(self, source, buffer, semaphore):
        self.copy, self.buffer, self.shape, self.here = pltpu.make_async_copy(source, buffer, semaphore), buffer, buffer.shape, False
        self.copy.start()

    def __getitem__(self, where):
        if not self.here:
            self.copy.wait()
            self.here = True
        return self.buffer[where]


def staged_call(kernel, outs, operands, scratch=(), scalars=(), flops=0, vmem=56):
    operands = [v if isinstance(v, tuple) else (v, None) for v in operands]
    ranges, operands = [v[1] for v in operands], [v[0] for v in operands]
    shapes = [v.shape if cols is None else (v.shape[0], cols[1] - cols[0]) for v, cols in zip(operands, ranges)]
    n, m = len(scalars), len(operands)

    def body(*refs):
        first, sources, rest = refs[:n], refs[n : n + m], refs[n + m :]
        results, rest = rest[: len(outs)], rest[len(outs) :]
        buffers, semaphores, rest = rest[:m], rest[m], rest[m + 1 :]
        sources = [v if cols is None else v.at[:, pl.ds(cols[0], cols[1] - cols[0])] for v, cols in zip(sources, ranges)]
        staged = [Staged(source, buffer, semaphores.at[t]) for t, (source, buffer) in enumerate(zip(sources, buffers))]
        kernel(*first, *staged, *results, *rest)

    return pl.pallas_call(
        body,
        out_shape=outs,
        in_specs=[pl.BlockSpec(memory_space=pltpu.SMEM)] * n + [pl.BlockSpec(memory_space=pl.ANY)] * m,
        out_specs=tuple(pl.BlockSpec(memory_space=pltpu.VMEM) for _ in outs),
        scratch_shapes=[pltpu.VMEM(dims, v.dtype) for v, dims in zip(operands, shapes)] + [pltpu.SemaphoreType.DMA((m,))] + list(scratch),
        compiler_params=pltpu.CompilerParams(vmem_limit_bytes=vmem << 20),
        cost_estimate=pl.CostEstimate(flops=flops, bytes_accessed=1 << 22, transcendentals=0),
    )(*scalars, *operands)


def shape(*dims, dtype=F32):
    return jax.ShapeDtypeStruct(dims, dtype)


def cut_kernel(pattern, a, c, k, by_x, own_z, fold, cw, m1, m2):
    row = lax.axis_index("row")

    def block_a(i, q):
        return a[pl.ds(i * 512 + q, W, stride=4), :]

    def block_k(j, q):
        return k[pl.ds(j * 256 + q, W, stride=2), :]

    def lay(out, *blocks):
        for n, block in enumerate(blocks):
            out[:, n * W : (n + 1) * W] = block

    lay(by_x, block_k(0, 0), block_k(1, 0), block_a(1, 0), block_a(1, 1))
    lay(own_z, block_a(1, 3), block_k(1, 1), block_a(1, 2), block_a(0, 0))
    lay(fold, block_a(0, 1), block_k(0, 1))
    for j in range(2):
        for i in range(2):
            kept = pattern[j, row + 16 * i].astype(F32)
            for q in range(2):
                block = c[pl.ds((j * 2 + i) * 256 + q, W, stride=2), :]
                cw[pl.ds((j * 2 + i) * W, W), q * W : (q + 1) * W] = block * kept
    even = row % 2 == 0
    for m, (i, q) in enumerate(((0, 0), (1, 0), (1, 2))):
        low, high = block_a(i, q).T, block_a(i, q + 1).T
        m1[pl.ds(m * W, W), :] = jnp.where(even, low, high)
        m2[pl.ds(m * W, W), :] = jnp.where(even, high, low)


def block_of(pieces, b, first, last):
    return pieces[b // 8][pl.ds((b % 8) * W, W), first * W : last * W]


def fold_home(b, x, z, core):
    from_z, from_x = origin(z, b % 4, core), origin(x, b // 4, core)
    kind = (from_x >= 2).astype(jnp.int32)
    return kind, jnp.where(from_x < 2, 1 - from_x, from_x - 2) * 4 + from_z


def update_kernel(*refs):
    cw, main, fold = refs[:2], refs[2:4], refs[4:6]
    outs, (high, low, rh, rl, eh, el) = refs[6:10], refs[10:]
    x, z, y, core = place()
    for w in range(8):
        column = column_of(w, y, core)
        for q in range(2):
            for j in range(2):
                block = cw[w // 4][pl.ds((w % 4) * 512 + j * 256, 256), q * W : (q + 1) * W]
                put(high, low, (j, slice(None), at(column + 8 * q, W)), block)
    for b in range(16):
        row = origin(x, b % 4, core) * 4 + origin(z, b // 4, core)
        put(rh, rl, (at(row, W), slice(None)), block_of(main, b, 0, 2))
        kind, row = fold_home(b, x, z, core)
        put(eh, el, (kind, at(row, W), slice(None)), block_of(fold, b, 1, 2))
    for j in range(2):
        cols = slice(j * W, (j + 1) * W)
        first = dot3((high[j], low[j]), (rh[:, cols], rl[:, cols]))
        upper = slice(1024, 2048)
        second = dot3((high[j, :, upper], low[j, :, upper]), (eh[j], el[j]))
        for i in range(2):
            outs[2 * j + i][:, :W] = first[i * W : (i + 1) * W]
            outs[2 * j + i][:, W:] = second[i * W : (i + 1) * W]


def root_kernel(*refs):
    m, by_x, by_z = refs[:2], refs[2:4], refs[4:6]
    (s_out, root_out), (h0, l0, h1, l1, rh, rl, r0h, r0l, eh, el) = refs[6:8], refs[8:]
    x, z, y, core = place()
    upper = (4 * x + z >= 8).astype(jnp.int32)
    for w in range(8):
        column = column_of(w, y, core)
        for n in range(2):
            here = at(2 * column + (n + upper) % 2, W)
            for part, (hr, lr, lo) in enumerate(((h0, l0, 0), (h1, l1, 0), (h1, l1, W))):
                block = m[w // 4][pl.ds(((w % 4) * 6 + n * 3 + part) * W, W), :]
                put(hr, lr, (pl.ds(lo, W), here), block)
    for b in range(16):
        row = origin(x, b % 4, core) * 4 + origin(z, b // 4, core)
        put(rh, rl, (at(row, W), slice(0, 2 * W)), block_of(by_x, b, 2, 4))
        row = origin(z, b % 4, core) + origin(x, b // 4, core) * 4
        block = block_of(by_z, b, 2, 4)
        put(rh, rl, (at(row, W), slice(2 * W, 3 * W)), block[:, :W])
        put(r0h, r0l, (at(row, W), slice(None)), block[:, W:])
        kind, row = fold_home(b, x, z, core)
        put(eh, el, (kind, at(row, W), slice(None)), block_of(by_z, b, 0, 1))
    late = slice(1024, 2048)
    s_out[:, : 3 * W] = dot3((h1[...], l1[...]), (rh[...], rl[...]))
    s_out[:, 3 * W :] = dot3((h1[:, late], l1[:, late]), (eh[1], el[1]))
    s_out[:W, :W] += dot3((h0[...], l0[...]), (r0h[...], r0l[...]))
    s_out[:W, W : 2 * W] += dot3((h0[:, late], l0[:, late]), (eh[0], el[0]))
    for i in range(2):
        for q in range(4):
            root_out[pl.ds(i * 512 + q, W, stride=4), :] = s_out[pl.ds(i * W, W), q * W : (q + 1) * W]


def order_kernel(*refs):
    s_in, (high, low) = refs[:2], refs[2:]
    x, z, y, core = place()
    for w in range(8):
        column = column_of(w, y, core)
        for q in range(4):
            row = column + 8 * (q % 2)
            along_x, along_z = step_of(row // 4, x, core), step_of(row % 4, z, core)
            block = along_x + 4 * along_z if q < 2 else 16 + along_z + 4 * along_x
            put(high, low, (slice(None), at(block, W)), s_in[w // 4][pl.ds((w % 4) * 256, 256), q * W : (q + 1) * W])


def halves_kernel(a, b, high, low):
    put(high, low, (slice(0, 1024), slice(None)), a[...])
    put(high, low, (slice(1024, 2048), slice(None)), b[...])


def early_kernel(high, low, near_high, near_low, total):
    first = dot3((high[:, :1024], low[:, :1024]), (near_high[:1024, :], near_low[:1024, :]))
    total[...] = first + dot3((high[:, 2048:3072], low[:, 2048:3072]), (near_high[1024:, :], near_low[1024:, :]))


def product_kernel(j, pattern, high, low, early, p0, p1, u0, u1, k, p_out, g_out):
    row = lax.axis_index("row")
    total = early[...] + dot3((high[:, 1024:2048], low[:, 1024:2048]), split(p0[...]))
    total = total + dot3((high[:, 3072:], low[:, 3072:]), split(p1[...]))
    scaled = [total[i * W : (i + 1) * W] * -pattern[j, row + 16 * i].astype(F32) for i in range(2)]
    for q in range(2):
        cols = slice(q * W, (q + 1) * W)
        own = k[pl.ds(j * 256 + q, W, stride=2), :]
        block = dot3(split(own.T), split(own))
        for i, u in enumerate((u0, u1)):
            p_out[pl.ds(i * 256 + q, W, stride=2), :] = scaled[i][:, cols]
            block = block - dot3(split(u[:, cols].T), split(scaled[i][:, cols]))
        g_out[pl.ds(q, W, stride=2), :] = block


def local(root_inverse, child_coupling, child_inverse, pattern):
    a = root_inverse.reshape(1024, W)
    c = child_coupling.reshape(1024, W)
    k = child_inverse.reshape(512, W)
    by_x, own_z, fold, cw, m1, m2 = staged_call(
        cut_kernel,
        (shape(W, 512), shape(W, 512), shape(W, 256), shape(512, 256), shape(384, W), shape(384, W)),
        (a, c, k),
        scalars=(pattern,),
    )

    folded = jnp.where(lax.axis_index("row") >= 8, own_z[:, : 2 * W], send(fold, FOLD))
    by_z = jnp.concatenate([folded, own_z[:, 2 * W :]], axis=1)
    x_parts, _ = gather(by_x, ALONG_X, ALONG_Z)
    z_parts, _ = gather(by_z, ALONG_Z, ALONG_X)
    coupling_parts = share(cw)
    u = call(
        update_kernel,
        (shape(W, 256),) * 4,
        scratch=[pltpu.VMEM((2, 256, 2048), BF16)] * 2 + [pltpu.VMEM((2048, 256), BF16)] * 2 + [pltpu.VMEM((2, 1024, W), BF16)] * 2,
        count=6,
        flops=1 << 31,
    )(*coupling_parts, *x_parts, *z_parts)

    mirrored = share(jnp.concatenate([send(m1, MIRROR_1), send(m2, MIRROR_2)], axis=0))
    panels, begun = [], []
    for j in range(2):
        (first, x_two), (second, z_two) = gather(u[2 * j], ALONG_X, ALONG_Z), gather(u[2 * j + 1], ALONG_Z, ALONG_X)
        panels.append((first, second))
        begun += [x_two, z_two]
    sigma, sigma_root = call(
        root_kernel,
        (shape(256, 512), shape(1024, W)),
        scratch=[pltpu.VMEM((W, 2048), BF16)] * 2
        + [pltpu.VMEM((256, 2048), BF16)] * 2
        + [pltpu.VMEM((2048, 384), BF16)] * 2
        + [pltpu.VMEM((2048, W), BF16)] * 2
        + [pltpu.VMEM((2, 1024, W), BF16)] * 2,
        count=6,
        flops=1 << 31,
    )(after(mirrored[0], *begun[:2]), mirrored[1], *x_parts, *z_parts)
    high, low = call(order_kernel, (shape(256, 4096, dtype=BF16),) * 2, count=2, flops=1 << 20)(*share(sigma))

    products, diagonals = [], []
    for j in range(2):
        u0, u1 = u[2 * j], u[2 * j + 1]
        first, second = panels[j]
        near = call(halves_kernel, (shape(2048, 256, dtype=BF16),) * 2, count=2, flops=HINT)(first[0], second[0])
        early = call(early_kernel, shape(256, 256), count=4, flops=1 << 30)(high, low, *near)
        p, g = call(
            functools.partial(product_kernel, j),
            (shape(512, W), shape(256, W)),
            smem_first=True,
            count=8,
            flops=1 << 30,
        )(pattern, high, low, early, first[1], second[1], u0, u1, k)
        for pairs in ALONG_X + ALONG_Z:
            g = g + send(g, pairs)
        diagonals.append(g)
        products.append(p)
    return (
        sigma_root.reshape(2, W, 4, W),
        jnp.concatenate(products).reshape(2, 2, W, 2, W),
        jnp.concatenate(diagonals).reshape(2, W, 2, W),
    )


def solution(mesh):
    in_specs = (
        P(None, "row", None, "col"),
        P(None, None, "row", None, "col"),
        P(None, None, "row", None, "col"),
        P(),
    )
    out_specs = (
        P(None, "row", None, "col"),
        P(None, None, "row", None, "col"),
        P(None, None, None, "col"),
    )
    return jax.shard_map(local, mesh=mesh, in_specs=in_specs, out_specs=out_specs, check_vma=False)
```

```python
import functools

import jax
import jax.numpy as jnp
from jax import lax
from jax.experimental import pallas as pl
from jax.experimental.pallas import tpu as pltpu
from jax.sharding import PartitionSpec as P

X, Z, Y, CORES = 4, 4, 4, 2
W = 128
HINT = 1 << 36
F32, BF16 = jnp.float32, jnp.bfloat16
AXES = ("row", "col")


def moves(target):
    pairs = []
    for x in range(X):
        for z in range(Z):
            for y in range(Y):
                for core in range(CORES):
                    there = target(x, z, y, core)
                    if there is not None:
                        u, w, v, k = there
                        pairs.append((((x * Z + z) * Y + y) * CORES + core, ((u * Z + w) * Y + v) * CORES + k))
    return pairs


FLIPS = ((1, 3), (3, 1))
ALONG_X = [moves(lambda x, z, y, k, n=n: (x ^ FLIPS[k][n], z, y, k)) for n in range(2)]
ALONG_Z = [moves(lambda x, z, y, k, n=n: (x, z ^ FLIPS[k][n], y, k)) for n in range(2)]
ALONG_Y = [moves(lambda x, z, y, k, n=n: (x, z, y ^ FLIPS[k][n], k)) for n in range(2)]
SWAP = moves(lambda x, z, y, k: (x, z, y, 1 - k))
FOLD = moves(lambda x, z, y, k: (3 - x, z, y, k) if x >= 2 else None)


def mirror(first):
    def target(x, z, y, k):
        r, c = x * Z + z, y * CORES + k
        to = c if (r % 2 == 0) == first else c + 8
        return to // Z, to % Z, (r // 2) // CORES, (r // 2) % CORES

    return moves(target)


MIRROR_1, MIRROR_2 = mirror(True), mirror(False)


def send(value, pairs):
    return lax.ppermute(value, AXES, pairs)


def both(value, pairs):
    return jnp.concatenate([value, send(value, pairs)], axis=0)


def after(value, *others):
    return lax.optimization_barrier((value, *others))[0]


def gather(value, first, second, *others):
    two = both(value, first[0])
    eight = both(both(two, first[1]), second[0])
    return [eight, send(after(eight, *others) if others else eight, second[1])], two


def share(value):
    four = both(both(value, ALONG_Y[0]), ALONG_Y[1])
    return [four, send(four, SWAP)]


def place():
    row, col = lax.axis_index("row"), lax.axis_index("col")
    return row // 4, row % 4, col // 2, col % 2


def origin(index, step, core):
    if step == 0:
        return index
    if step == 3:
        return index ^ 2
    return index ^ jnp.where(core == step - 1, 1, 3)


def step_of(there, here, core):
    flip = there ^ here
    swapped = jnp.where(flip == 0, 0, jnp.where(flip == 2, 3, jnp.where(flip == 1, 1, 2)))
    return jnp.where((core == 1) & ((flip == 1) | (flip == 3)), 3 - swapped, swapped)


def column_of(w, y, core):
    owner = core if w < 4 else 1 - core
    return 2 * origin(y, w % 4, owner) + owner


def at(index, size):
    return pl.ds(pl.multiple_of(index * size, size), size)


def split(value):
    high = value.astype(BF16)
    return high, (value - high.astype(F32)).astype(BF16)


def put(high, low, where, value):
    h, l = split(value)
    high[where] = h
    low[where] = l


def dot3(left, right):
    dot = functools.partial(jnp.dot, preferred_element_type=F32)
    return dot(left[0], right[0]) + (dot(left[0], right[1]) + dot(left[1], right[0]))


def call(kernel, outs, scratch=(), smem_first=False, count=0, flops=0, vmem=24):
    in_specs = [pl.BlockSpec(memory_space=pltpu.VMEM)] * count
    if smem_first:
        in_specs = [pl.BlockSpec(memory_space=pltpu.SMEM)] + in_specs
    return pl.pallas_call(
        kernel,
        out_shape=outs,
        in_specs=in_specs,
        out_specs=jax.tree.map(lambda _: pl.BlockSpec(memory_space=pltpu.VMEM), outs),
        scratch_shapes=list(scratch),
        compiler_params=pltpu.CompilerParams(vmem_limit_bytes=vmem << 20),
        cost_estimate=pl.CostEstimate(flops=flops, bytes_accessed=1 << 22, transcendentals=0),
    )


class Staged:
    def __init__(self, source, buffer, semaphore):
        self.copy, self.buffer, self.shape, self.here = pltpu.make_async_copy(source, buffer, semaphore), buffer, buffer.shape, False
        self.copy.start()

    def __getitem__(self, where):
        if not self.here:
            self.copy.wait()
            self.here = True
        return self.buffer[where]


def staged_call(kernel, outs, operands, scratch=(), scalars=(), flops=0, vmem=56):
    operands = [v if isinstance(v, tuple) else (v, None) for v in operands]
    ranges, operands = [v[1] for v in operands], [v[0] for v in operands]
    shapes = [v.shape if cols is None else (v.shape[0], cols[1] - cols[0]) for v, cols in zip(operands, ranges)]
    n, m = len(scalars), len(operands)

    def body(*refs):
        first, sources, rest = refs[:n], refs[n : n + m], refs[n + m :]
        results, rest = rest[: len(outs)], rest[len(outs) :]
        buffers, semaphores, rest = rest[:m], rest[m], rest[m + 1 :]
        sources = [v if cols is None else v.at[:, pl.ds(cols[0], cols[1] - cols[0])] for v, cols in zip(sources, ranges)]
        staged = [Staged(source, buffer, semaphores.at[t]) for t, (source, buffer) in enumerate(zip(sources, buffers))]
        kernel(*first, *staged, *results, *rest)

    return pl.pallas_call(
        body,
        out_shape=outs,
        in_specs=[pl.BlockSpec(memory_space=pltpu.SMEM)] * n + [pl.BlockSpec(memory_space=pl.ANY)] * m,
        out_specs=tuple(pl.BlockSpec(memory_space=pltpu.VMEM) for _ in outs),
        scratch_shapes=[pltpu.VMEM(dims, v.dtype) for v, dims in zip(operands, shapes)] + [pltpu.SemaphoreType.DMA((m,))] + list(scratch),
        compiler_params=pltpu.CompilerParams(vmem_limit_bytes=vmem << 20),
        cost_estimate=pl.CostEstimate(flops=flops, bytes_accessed=1 << 22, transcendentals=0),
    )(*scalars, *operands)


def shape(*dims, dtype=F32):
    return jax.ShapeDtypeStruct(dims, dtype)


def cut_kernel(pattern, a, c, k, by_x, own_z, fold, cw, m1, m2):
    row = lax.axis_index("row")

    def block_a(i, q):
        return a[pl.ds(i * 512 + q, W, stride=4), :]

    def block_k(j, q):
        return k[pl.ds(j * 256 + q, W, stride=2), :]

    def lay(out, *blocks):
        for n, block in enumerate(blocks):
            out[:, n * W : (n + 1) * W] = block

    lay(by_x, block_k(0, 0), block_k(1, 0), block_a(1, 0), block_a(1, 1))
    lay(own_z, block_a(1, 3), block_k(1, 1), block_a(1, 2), block_a(0, 0))
    lay(fold, block_a(0, 1), block_k(0, 1))
    for j in range(2):
        for i in range(2):
            kept = pattern[j, row + 16 * i].astype(F32)
            for q in range(2):
                block = c[pl.ds((j * 2 + i) * 256 + q, W, stride=2), :]
                cw[pl.ds((j * 2 + i) * W, W), q * W : (q + 1) * W] = block * kept
    even = row % 2 == 0
    for m, (i, q) in enumerate(((0, 0), (1, 0), (1, 2))):
        low, high = block_a(i, q).T, block_a(i, q + 1).T
        m1[pl.ds(m * W, W), :] = jnp.where(even, low, high)
        m2[pl.ds(m * W, W), :] = jnp.where(even, high, low)


def block_of(pieces, b, first, last):
    return pieces[b // 8][pl.ds((b % 8) * W, W), first * W : last * W]


def fold_home(b, x, z, core):
    from_z, from_x = origin(z, b % 4, core), origin(x, b // 4, core)
    kind = (from_x >= 2).astype(jnp.int32)
    return kind, jnp.where(from_x < 2, 1 - from_x, from_x - 2) * 4 + from_z


def update_kernel(*refs):
    cw, main, fold = refs[:2], refs[2:4], refs[4:6]
    outs, (high, low, rh, rl, eh, el) = refs[6:10], refs[10:]
    x, z, y, core = place()
    for w in range(8):
        column = column_of(w, y, core)
        for q in range(2):
            for j in range(2):
                block = cw[w // 4][pl.ds((w % 4) * 512 + j * 256, 256), q * W : (q + 1) * W]
                put(high, low, (j, slice(None), at(column + 8 * q, W)), block)
    for b in range(16):
        row = origin(x, b % 4, core) * 4 + origin(z, b // 4, core)
        put(rh, rl, (at(row, W), slice(None)), block_of(main, b, 0, 2))
        kind, row = fold_home(b, x, z, core)
        put(eh, el, (kind, at(row, W), slice(None)), block_of(fold, b, 1, 2))
    for j in range(2):
        cols = slice(j * W, (j + 1) * W)
        first = dot3((high[j], low[j]), (rh[:, cols], rl[:, cols]))
        upper = slice(1024, 2048)
        second = dot3((high[j, :, upper], low[j, :, upper]), (eh[j], el[j]))
        for i in range(2):
            outs[2 * j + i][:, :W] = first[i * W : (i + 1) * W]
            outs[2 * j + i][:, W:] = second[i * W : (i + 1) * W]


def root_kernel(*refs):
    m, by_x, by_z = refs[:2], refs[2:4], refs[4:6]
    (s_out, root_out), (h0, l0, h1, l1, rh, rl, r0h, r0l, eh, el) = refs[6:8], refs[8:]
    x, z, y, core = place()
    upper = (4 * x + z >= 8).astype(jnp.int32)
    for w in range(8):
        column = column_of(w, y, core)
        for n in range(2):
            here = at(2 * column + (n + upper) % 2, W)
            for part, (hr, lr, lo) in enumerate(((h0, l0, 0), (h1, l1, 0), (h1, l1, W))):
                block = m[w // 4][pl.ds(((w % 4) * 6 + n * 3 + part) * W, W), :]
                put(hr, lr, (pl.ds(lo, W), here), block)
    for b in range(16):
        row = origin(x, b % 4, core) * 4 + origin(z, b // 4, core)
        put(rh, rl, (at(row, W), slice(0, 2 * W)), block_of(by_x, b, 2, 4))
        row = origin(z, b % 4, core) + origin(x, b // 4, core) * 4
        block = block_of(by_z, b, 2, 4)
        put(rh, rl, (at(row, W), slice(2 * W, 3 * W)), block[:, :W])
        put(r0h, r0l, (at(row, W), slice(None)), block[:, W:])
        kind, row = fold_home(b, x, z, core)
        put(eh, el, (kind, at(row, W), slice(None)), block_of(by_z, b, 0, 1))
    late = slice(1024, 2048)
    s_out[:, : 3 * W] = dot3((h1[...], l1[...]), (rh[...], rl[...]))
    s_out[:, 3 * W :] = dot3((h1[:, late], l1[:, late]), (eh[1], el[1]))
    s_out[:W, :W] += dot3((h0[...], l0[...]), (r0h[...], r0l[...]))
    s_out[:W, W : 2 * W] += dot3((h0[:, late], l0[:, late]), (eh[0], el[0]))
    for i in range(2):
        for q in range(4):
            root_out[pl.ds(i * 512 + q, W, stride=4), :] = s_out[pl.ds(i * W, W), q * W : (q + 1) * W]


def order_kernel(*refs):
    s_in, (high, low) = refs[:2], refs[2:]
    x, z, y, core = place()
    for w in range(8):
        column = column_of(w, y, core)
        for q in range(4):
            row = column + 8 * (q % 2)
            along_x, along_z = step_of(row // 4, x, core), step_of(row % 4, z, core)
            block = along_x + 4 * along_z if q < 2 else 16 + along_z + 4 * along_x
            put(high, low, (slice(None), at(block, W)), s_in[w // 4][pl.ds((w % 4) * 256, 256), q * W : (q + 1) * W])


def halves_kernel(a, b, high, low):
    put(high, low, (slice(0, 1024), slice(None)), a[...])
    put(high, low, (slice(1024, 2048), slice(None)), b[...])


def early_kernel(high, low, near_high, near_low, total):
    first = dot3((high[:, :1024], low[:, :1024]), (near_high[:1024, :], near_low[:1024, :]))
    total[...] = first + dot3((high[:, 2048:3072], low[:, 2048:3072]), (near_high[1024:, :], near_low[1024:, :]))


def product_kernel(j, pattern, high, low, early, p0, p1, u0, u1, k, p_out, g_out):
    row = lax.axis_index("row")
    total = early[...] + dot3((high[:, 1024:2048], low[:, 1024:2048]), split(p0[...]))
    total = total + dot3((high[:, 3072:], low[:, 3072:]), split(p1[...]))
    scaled = [total[i * W : (i + 1) * W] * -pattern[j, row + 16 * i].astype(F32) for i in range(2)]
    for q in range(2):
        cols = slice(q * W, (q + 1) * W)
        own = k[pl.ds(j * 256 + q, W, stride=2), :]
        block = dot3(split(own.T), split(own))
        for i, u in enumerate((u0, u1)):
            p_out[pl.ds(i * 256 + q, W, stride=2), :] = scaled[i][:, cols]
            block = block - dot3(split(u[:, cols].T), split(scaled[i][:, cols]))
        g_out[pl.ds(q, W, stride=2), :] = block


def local(root_inverse, child_coupling, child_inverse, pattern):
    a = root_inverse.reshape(1024, W)
    c = child_coupling.reshape(1024, W)
    k = child_inverse.reshape(512, W)
    by_x, own_z, fold, cw, m1, m2 = staged_call(
        cut_kernel,
        (shape(W, 512), shape(W, 512), shape(W, 256), shape(512, 256), shape(384, W), shape(384, W)),
        (a, c, k),
        scalars=(pattern,),
    )

    folded = jnp.where(lax.axis_index("row") >= 8, own_z[:, : 2 * W], send(fold, FOLD))
    by_z = jnp.concatenate([folded, own_z[:, 2 * W :]], axis=1)
    m1, m2 = send(m1, MIRROR_1), send(m2, MIRROR_2)
    x_parts, _ = gather(by_x, ALONG_X, ALONG_Z, m1, m2)
    z_parts, _ = gather(by_z, ALONG_Z, ALONG_X, m1, m2)
    coupling_parts = share(cw)
    u = call(
        update_kernel,
        (shape(W, 256),) * 4,
        scratch=[pltpu.VMEM((2, 256, 2048), BF16)] * 2 + [pltpu.VMEM((2048, 256), BF16)] * 2 + [pltpu.VMEM((2, 1024, W), BF16)] * 2,
        count=6,
        flops=HINT,
    )(*coupling_parts, *x_parts, *z_parts)

    mirrored = share(jnp.concatenate([m1, m2], axis=0))
    panels, begun = [], []
    for j in range(2):
        (first, x_two), (second, z_two) = gather(u[2 * j], ALONG_X, ALONG_Z), gather(u[2 * j + 1], ALONG_Z, ALONG_X)
        panels.append((first, second))
        begun += [x_two, z_two]
    sigma, sigma_root = call(
        root_kernel,
        (shape(256, 512), shape(1024, W)),
        scratch=[pltpu.VMEM((W, 2048), BF16)] * 2
        + [pltpu.VMEM((256, 2048), BF16)] * 2
        + [pltpu.VMEM((2048, 384), BF16)] * 2
        + [pltpu.VMEM((2048, W), BF16)] * 2
        + [pltpu.VMEM((2, 1024, W), BF16)] * 2,
        count=6,
        flops=1 << 31,
    )(after(mirrored[0], *begun[:2]), mirrored[1], *x_parts, *z_parts)
    high, low = call(order_kernel, (shape(256, 4096, dtype=BF16),) * 2, count=2, flops=1 << 20)(*share(sigma))

    products, diagonals = [], []
    for j in range(2):
        u0, u1 = u[2 * j], u[2 * j + 1]
        first, second = panels[j]
        near = call(halves_kernel, (shape(2048, 256, dtype=BF16),) * 2, count=2, flops=HINT)(first[0], second[0])
        early = call(early_kernel, shape(256, 256), count=4, flops=1 << 30)(high, low, *near)
        p, g = call(
            functools.partial(product_kernel, j),
            (shape(512, W), shape(256, W)),
            smem_first=True,
            count=8,
            flops=1 << 30,
        )(pattern, high, low, early, first[1], second[1], u0, u1, k)
        for pairs in ALONG_X + ALONG_Z:
            g = g + send(g, pairs)
        diagonals.append(g)
        products.append(p)
    return (
        sigma_root.reshape(2, W, 4, W),
        jnp.concatenate(products).reshape(2, 2, W, 2, W),
        jnp.concatenate(diagonals).reshape(2, W, 2, W),
    )


def solution(mesh):
    in_specs = (
        P(None, "row", None, "col"),
        P(None, None, "row", None, "col"),
        P(None, None, "row", None, "col"),
        P(),
    )
    out_specs = (
        P(None, "row", None, "col"),
        P(None, None, "row", None, "col"),
        P(None, None, None, "col"),
    )
    return jax.shard_map(local, mesh=mesh, in_specs=in_specs, out_specs=out_specs, check_vma=False)
```

```python
import functools

import jax
import jax.numpy as jnp
from jax import lax
from jax.experimental import pallas as pl
from jax.experimental.pallas import tpu as pltpu
from jax.sharding import PartitionSpec as P

X, Z, Y, CORES = 4, 4, 4, 2
W = 128
HINT = 1 << 36
F32, BF16 = jnp.float32, jnp.bfloat16
AXES = ("row", "col")


def moves(target):
    pairs = []
    for x in range(X):
        for z in range(Z):
            for y in range(Y):
                for core in range(CORES):
                    there = target(x, z, y, core)
                    if there is not None:
                        u, w, v, k = there
                        pairs.append((((x * Z + z) * Y + y) * CORES + core, ((u * Z + w) * Y + v) * CORES + k))
    return pairs


FLIPS = ((1, 3), (3, 1))
ALONG_X = [moves(lambda x, z, y, k, n=n: (x ^ FLIPS[k][n], z, y, k)) for n in range(2)]
ALONG_Z = [moves(lambda x, z, y, k, n=n: (x, z ^ FLIPS[k][n], y, k)) for n in range(2)]
ALONG_Y = [moves(lambda x, z, y, k, n=n: (x, z, y ^ FLIPS[k][n], k)) for n in range(2)]
SWAP = moves(lambda x, z, y, k: (x, z, y, 1 - k))
FOLD = moves(lambda x, z, y, k: (3 - x, z, y, k) if x >= 2 else None)


def mirror(first):
    def target(x, z, y, k):
        r, c = x * Z + z, y * CORES + k
        to = c if (r % 2 == 0) == first else c + 8
        return to // Z, to % Z, (r // 2) // CORES, (r // 2) % CORES

    return moves(target)


MIRROR_1, MIRROR_2 = mirror(True), mirror(False)


def send(value, pairs):
    return lax.ppermute(value, AXES, pairs)


def both(value, pairs):
    return jnp.concatenate([value, send(value, pairs)], axis=0)


def after(value, *others):
    return lax.optimization_barrier((value, *others))[0]


def gather(value, first, second, *others):
    two = both(value, first[0])
    eight = both(both(two, first[1]), second[0])
    return [eight, send(after(eight, *others) if others else eight, second[1])], two


def share(value, *others):
    four = both(both(value, ALONG_Y[0]), ALONG_Y[1])
    return [four, send(after(four, *others) if others else four, SWAP)]


def place():
    row, col = lax.axis_index("row"), lax.axis_index("col")
    return row // 4, row % 4, col // 2, col % 2


def origin(index, step, core):
    if step == 0:
        return index
    if step == 3:
        return index ^ 2
    return index ^ jnp.where(core == step - 1, 1, 3)


def step_of(there, here, core):
    flip = there ^ here
    swapped = jnp.where(flip == 0, 0, jnp.where(flip == 2, 3, jnp.where(flip == 1, 1, 2)))
    return jnp.where((core == 1) & ((flip == 1) | (flip == 3)), 3 - swapped, swapped)


def column_of(w, y, core):
    owner = core if w < 4 else 1 - core
    return 2 * origin(y, w % 4, owner) + owner


def at(index, size):
    return pl.ds(pl.multiple_of(index * size, size), size)


def split(value):
    high = value.astype(BF16)
    return high, (value - high.astype(F32)).astype(BF16)


def put(high, low, where, value):
    h, l = split(value)
    high[where] = h
    low[where] = l


def dot3(left, right):
    dot = functools.partial(jnp.dot, preferred_element_type=F32)
    return dot(left[0], right[0]) + (dot(left[0], right[1]) + dot(left[1], right[0]))


def call(kernel, outs, scratch=(), smem_first=False, count=0, flops=0, vmem=24):
    in_specs = [pl.BlockSpec(memory_space=pltpu.VMEM)] * count
    if smem_first:
        in_specs = [pl.BlockSpec(memory_space=pltpu.SMEM)] + in_specs
    return pl.pallas_call(
        kernel,
        out_shape=outs,
        in_specs=in_specs,
        out_specs=jax.tree.map(lambda _: pl.BlockSpec(memory_space=pltpu.VMEM), outs),
        scratch_shapes=list(scratch),
        compiler_params=pltpu.CompilerParams(vmem_limit_bytes=vmem << 20),
        cost_estimate=pl.CostEstimate(flops=flops, bytes_accessed=1 << 22, transcendentals=0),
    )


class Staged:
    def __init__(self, source, buffer, semaphore):
        self.copy, self.buffer, self.shape, self.here = pltpu.make_async_copy(source, buffer, semaphore), buffer, buffer.shape, False
        self.copy.start()

    def __getitem__(self, where):
        if not self.here:
            self.copy.wait()
            self.here = True
        return self.buffer[where]


def staged_call(kernel, outs, operands, scratch=(), scalars=(), flops=0, vmem=56):
    operands = [v if isinstance(v, tuple) else (v, None) for v in operands]
    ranges, operands = [v[1] for v in operands], [v[0] for v in operands]
    shapes = [v.shape if cols is None else (v.shape[0], cols[1] - cols[0]) for v, cols in zip(operands, ranges)]
    n, m = len(scalars), len(operands)

    def body(*refs):
        first, sources, rest = refs[:n], refs[n : n + m], refs[n + m :]
        results, rest = rest[: len(outs)], rest[len(outs) :]
        buffers, semaphores, rest = rest[:m], rest[m], rest[m + 1 :]
        sources = [v if cols is None else v.at[:, pl.ds(cols[0], cols[1] - cols[0])] for v, cols in zip(sources, ranges)]
        staged = [Staged(source, buffer, semaphores.at[t]) for t, (source, buffer) in enumerate(zip(sources, buffers))]
        kernel(*first, *staged, *results, *rest)

    return pl.pallas_call(
        body,
        out_shape=outs,
        in_specs=[pl.BlockSpec(memory_space=pltpu.SMEM)] * n + [pl.BlockSpec(memory_space=pl.ANY)] * m,
        out_specs=tuple(pl.BlockSpec(memory_space=pltpu.VMEM) for _ in outs),
        scratch_shapes=[pltpu.VMEM(dims, v.dtype) for v, dims in zip(operands, shapes)] + [pltpu.SemaphoreType.DMA((m,))] + list(scratch),
        compiler_params=pltpu.CompilerParams(vmem_limit_bytes=vmem << 20),
        cost_estimate=pl.CostEstimate(flops=flops, bytes_accessed=1 << 22, transcendentals=0),
    )(*scalars, *operands)


def shape(*dims, dtype=F32):
    return jax.ShapeDtypeStruct(dims, dtype)


def cut_kernel(pattern, a, c, k, by_x, own_z, fold, cw, m1, m2):
    row = lax.axis_index("row")

    def block_a(i, q):
        return a[pl.ds(i * 512 + q, W, stride=4), :]

    def block_k(j, q):
        return k[pl.ds(j * 256 + q, W, stride=2), :]

    def lay(out, *blocks):
        for n, block in enumerate(blocks):
            out[:, n * W : (n + 1) * W] = block

    lay(by_x, block_k(0, 0), block_k(1, 0), block_a(1, 0), block_a(1, 1))
    lay(own_z, block_a(1, 3), block_k(1, 1), block_a(1, 2), block_a(0, 0))
    lay(fold, block_a(0, 1), block_k(0, 1))
    for j in range(2):
        for i in range(2):
            kept = pattern[j, row + 16 * i].astype(F32)
            for q in range(2):
                block = c[pl.ds((j * 2 + i) * 256 + q, W, stride=2), :]
                cw[pl.ds((j * 2 + i) * W, W), q * W : (q + 1) * W] = block * kept
    even = row % 2 == 0
    for m, (i, q) in enumerate(((0, 0), (1, 0), (1, 2))):
        low, high = block_a(i, q).T, block_a(i, q + 1).T
        m1[pl.ds(m * W, W), :] = jnp.where(even, low, high)
        m2[pl.ds(m * W, W), :] = jnp.where(even, high, low)


def block_of(pieces, b, first, last):
    return pieces[b // 8][pl.ds((b % 8) * W, W), first * W : last * W]


def fold_home(b, x, z, core):
    from_z, from_x = origin(z, b % 4, core), origin(x, b // 4, core)
    kind = (from_x >= 2).astype(jnp.int32)
    return kind, jnp.where(from_x < 2, 1 - from_x, from_x - 2) * 4 + from_z


def update_kernel(*refs):
    cw, main, fold = refs[:2], refs[2:4], refs[4:6]
    outs, (high, low, rh, rl, eh, el) = refs[6:10], refs[10:]
    x, z, y, core = place()
    for w in range(8):
        column = column_of(w, y, core)
        for q in range(2):
            for j in range(2):
                block = cw[w // 4][pl.ds((w % 4) * 512 + j * 256, 256), q * W : (q + 1) * W]
                put(high, low, (j, slice(None), at(column + 8 * q, W)), block)
    for b in range(16):
        row = origin(x, b % 4, core) * 4 + origin(z, b // 4, core)
        put(rh, rl, (at(row, W), slice(None)), block_of(main, b, 0, 2))
        kind, row = fold_home(b, x, z, core)
        put(eh, el, (kind, at(row, W), slice(None)), block_of(fold, b, 1, 2))
    for j in range(2):
        cols = slice(j * W, (j + 1) * W)
        first = dot3((high[j], low[j]), (rh[:, cols], rl[:, cols]))
        upper = slice(1024, 2048)
        second = dot3((high[j, :, upper], low[j, :, upper]), (eh[j], el[j]))
        for i in range(2):
            outs[2 * j + i][:, :W] = first[i * W : (i + 1) * W]
            outs[2 * j + i][:, W:] = second[i * W : (i + 1) * W]


def root_kernel(*refs):
    m, by_x, by_z = refs[:2], refs[2:4], refs[4:6]
    (s_out, root_out), (h0, l0, h1, l1, rh, rl, r0h, r0l, eh, el) = refs[6:8], refs[8:]
    x, z, y, core = place()
    upper = (4 * x + z >= 8).astype(jnp.int32)
    for w in range(8):
        column = column_of(w, y, core)
        for n in range(2):
            here = at(2 * column + (n + upper) % 2, W)
            for part, (hr, lr, lo) in enumerate(((h0, l0, 0), (h1, l1, 0), (h1, l1, W))):
                block = m[w // 4][pl.ds(((w % 4) * 6 + n * 3 + part) * W, W), :]
                put(hr, lr, (pl.ds(lo, W), here), block)
    for b in range(16):
        row = origin(x, b % 4, core) * 4 + origin(z, b // 4, core)
        put(rh, rl, (at(row, W), slice(0, 2 * W)), block_of(by_x, b, 2, 4))
        row = origin(z, b % 4, core) + origin(x, b // 4, core) * 4
        block = block_of(by_z, b, 2, 4)
        put(rh, rl, (at(row, W), slice(2 * W, 3 * W)), block[:, :W])
        put(r0h, r0l, (at(row, W), slice(None)), block[:, W:])
        kind, row = fold_home(b, x, z, core)
        put(eh, el, (kind, at(row, W), slice(None)), block_of(by_z, b, 0, 1))
    late = slice(1024, 2048)
    s_out[:, : 3 * W] = dot3((h1[...], l1[...]), (rh[...], rl[...]))
    s_out[:, 3 * W :] = dot3((h1[:, late], l1[:, late]), (eh[1], el[1]))
    s_out[:W, :W] += dot3((h0[...], l0[...]), (r0h[...], r0l[...]))
    s_out[:W, W : 2 * W] += dot3((h0[:, late], l0[:, late]), (eh[0], el[0]))
    for i in range(2):
        for q in range(4):
            root_out[pl.ds(i * 512 + q, W, stride=4), :] = s_out[pl.ds(i * W, W), q * W : (q + 1) * W]


def order_kernel(*refs):
    s_in, (high, low) = refs[:2], refs[2:]
    x, z, y, core = place()
    for w in range(8):
        column = column_of(w, y, core)
        for q in range(4):
            row = column + 8 * (q % 2)
            along_x, along_z = step_of(row // 4, x, core), step_of(row % 4, z, core)
            block = along_x + 4 * along_z if q < 2 else 16 + along_z + 4 * along_x
            put(high, low, (slice(None), at(block, W)), s_in[w // 4][pl.ds((w % 4) * 256, 256), q * W : (q + 1) * W])


def halves_kernel(a, b, high, low):
    put(high, low, (slice(0, 1024), slice(None)), a[...])
    put(high, low, (slice(1024, 2048), slice(None)), b[...])


def early_kernel(high, low, near_high, near_low, total):
    first = dot3((high[:, :1024], low[:, :1024]), (near_high[:1024, :], near_low[:1024, :]))
    total[...] = first + dot3((high[:, 2048:3072], low[:, 2048:3072]), (near_high[1024:, :], near_low[1024:, :]))


def product_kernel(j, pattern, high, low, early, p0, p1, u0, u1, k, p_out, g_out):
    row = lax.axis_index("row")
    total = early[...] + dot3((high[:, 1024:2048], low[:, 1024:2048]), split(p0[...]))
    total = total + dot3((high[:, 3072:], low[:, 3072:]), split(p1[...]))
    scaled = [total[i * W : (i + 1) * W] * -pattern[j, row + 16 * i].astype(F32) for i in range(2)]
    for q in range(2):
        cols = slice(q * W, (q + 1) * W)
        own = k[pl.ds(j * 256 + q, W, stride=2), :]
        block = dot3(split(own.T), split(own))
        for i, u in enumerate((u0, u1)):
            p_out[pl.ds(i * 256 + q, W, stride=2), :] = scaled[i][:, cols]
            block = block - dot3(split(u[:, cols].T), split(scaled[i][:, cols]))
        g_out[pl.ds(q, W, stride=2), :] = block


def local(root_inverse, child_coupling, child_inverse, pattern):
    a = root_inverse.reshape(1024, W)
    c = child_coupling.reshape(1024, W)
    k = child_inverse.reshape(512, W)
    by_x, own_z, fold, cw, m1, m2 = staged_call(
        cut_kernel,
        (shape(W, 512), shape(W, 512), shape(W, 256), shape(512, 256), shape(384, W), shape(384, W)),
        (a, c, k),
        scalars=(pattern,),
    )

    folded = jnp.where(lax.axis_index("row") >= 8, own_z[:, : 2 * W], send(fold, FOLD))
    by_z = jnp.concatenate([folded, own_z[:, 2 * W :]], axis=1)
    m1, m2 = send(m1, MIRROR_1), send(m2, MIRROR_2)
    x_parts, _ = gather(by_x, ALONG_X, ALONG_Z, m1, m2)
    z_parts, _ = gather(by_z, ALONG_Z, ALONG_X, m1, m2)
    coupling_parts = share(cw, x_parts[0], z_parts[0], m1, m2)
    u = call(
        update_kernel,
        (shape(W, 256),) * 4,
        scratch=[pltpu.VMEM((2, 256, 2048), BF16)] * 2 + [pltpu.VMEM((2048, 256), BF16)] * 2 + [pltpu.VMEM((2, 1024, W), BF16)] * 2,
        count=6,
        flops=HINT,
    )(*coupling_parts, *x_parts, *z_parts)

    mirrored = share(jnp.concatenate([m1, m2], axis=0))
    panels, begun = [], []
    for j in range(2):
        (first, x_two), (second, z_two) = gather(u[2 * j], ALONG_X, ALONG_Z), gather(u[2 * j + 1], ALONG_Z, ALONG_X)
        panels.append((first, second))
        begun += [x_two, z_two]
    sigma, sigma_root = call(
        root_kernel,
        (shape(256, 512), shape(1024, W)),
        scratch=[pltpu.VMEM((W, 2048), BF16)] * 2
        + [pltpu.VMEM((256, 2048), BF16)] * 2
        + [pltpu.VMEM((2048, 384), BF16)] * 2
        + [pltpu.VMEM((2048, W), BF16)] * 2
        + [pltpu.VMEM((2, 1024, W), BF16)] * 2,
        count=6,
        flops=1 << 31,
    )(after(mirrored[0], *begun[:2]), mirrored[1], *x_parts, *z_parts)
    high, low = call(order_kernel, (shape(256, 4096, dtype=BF16),) * 2, count=2, flops=1 << 20)(*share(sigma))

    products, diagonals = [], []
    for j in range(2):
        u0, u1 = u[2 * j], u[2 * j + 1]
        first, second = panels[j]
        near = call(halves_kernel, (shape(2048, 256, dtype=BF16),) * 2, count=2, flops=HINT)(first[0], second[0])
        early = call(early_kernel, shape(256, 256), count=4, flops=1 << 30)(high, low, *near)
        p, g = call(
            functools.partial(product_kernel, j),
            (shape(512, W), shape(256, W)),
            smem_first=True,
            count=8,
            flops=1 << 30,
        )(pattern, high, low, early, first[1], second[1], u0, u1, k)
        for pairs in ALONG_X + ALONG_Z:
            g = g + send(g, pairs)
        diagonals.append(g)
        products.append(p)
    return (
        sigma_root.reshape(2, W, 4, W),
        jnp.concatenate(products).reshape(2, 2, W, 2, W),
        jnp.concatenate(diagonals).reshape(2, W, 2, W),
    )


def solution(mesh):
    in_specs = (
        P(None, "row", None, "col"),
        P(None, None, "row", None, "col"),
        P(None, None, "row", None, "col"),
        P(),
    )
    out_specs = (
        P(None, "row", None, "col"),
        P(None, None, "row", None, "col"),
        P(None, None, None, "col"),
    )
    return jax.shard_map(local, mesh=mesh, in_specs=in_specs, out_specs=out_specs, check_vma=False)
```
